768 devices in a mesh: row: 16 (over y, core), col: 8 (over z_hi, x), depth: 6 (over z_lo).
Axes of the slice: x: 4, y: 8, z: 12 (z_hi: 2, z_lo: 6; z = z_hi * 6 + z_lo), core: 2. Of those that a mesh axis runs over, the one named last changes fastest.
Arguments:
- propagation: bfloat16 [6, 2048, 49152], P('depth', 'col', 'row'), may hold values from -0.21875 to 0.21875
- tile_mask: int32 [6, 16, 384], P('depth', 'col', 'row'), may hold values from 0 to 1
- features: bfloat16 [6, 2048, 256], P('depth', 'col', 'row'), may hold values from -6 to 6
- teleport: bfloat16 [49152, 256], P(('row', 'col', 'depth')), may hold values from -6 to 6
Outputs:
- logits: float32 [49152, 256], P(('row', 'col', 'depth'))
The draws below stay inside these ranges and needn't reach their ends.
All inputs are finite; a program needn't handle non-finite values.
Results may differ from the reference program's by a relative error of at most 0.0003.
Values may be sent and summed in bfloat16 or wider, within the bound.
No kernel may reach another device: no remote copies, remote signals or barrier semaphores. Data moves between devices by JAX's collectives and lax.ppermute only.
A program may use at most 32 MiB of HBM per device.

```python
import jax
import jax.numpy as jnp
from jax import lax

C = 256
SLAB = 2048
N = 49152
INNER = 12288
N_DEPTH = 6


def draw_tile_mask(key, part):
    key = jax.random.fold_in(key, 7)
    level_key, live_key = jax.random.split(key)
    levels = jax.random.randint(level_key, (N // 128,), 0, 3)
    rates = jnp.left_shift(jnp.full((N // 128,), 2, jnp.int32), levels.astype(jnp.int32))
    draws = jax.random.randint(live_key, (N_DEPTH, SLAB // 128, N // 128), 0, 32)
    return (draws < rates[None, None, :]).astype(jnp.int32)


def spiked(result, key, source, target, shards_of, factor):
    def block_of(dim):
        return (jnp.arange(result.shape[dim]) // (result.shape[dim] // shards_of)).reshape((-1,) + (1,) * (result.ndim - 1 - dim))

    near = jax.random.permutation(key, shards_of)[block_of(target)]
    far = (block_of(target) + shards_of // 2) % shards_of
    return jnp.where((block_of(source) == near) | (block_of(source) == far), factor * result, result)


def level_of(rng, shape, cuts, low, largest):
    def one(position, shards_of):
        heights = jax.random.uniform(jax.random.fold_in(jax.random.fold_in(rng, 6), position), (shards_of,), jnp.float32, low / len(cuts), largest / len(cuts))
        return jnp.repeat(jnp.exp(heights), shape[position] // shards_of).reshape((-1,) + (1,) * (len(shape) - position - 1))

    factor_of = one(*cuts[0])
    for cut in cuts[1:]:
        factor_of = factor_of * one(*cut)
    return factor_of


def gaussian(stream_key, dims, scale, most, pieces=(), dtype=jnp.bfloat16):
    drawn = scale * jax.random.normal(stream_key, dims, jnp.float32)
    if pieces:
        drawn = drawn * level_of(stream_key, dims, pieces, -0.22, 0.18)
    return jnp.clip(drawn, -most, most).astype(dtype)


def noise_with(own_key, extent, width, reach, cuts, heavy, dtype=jnp.bfloat16):
    drawn = width * jax.random.normal(own_key, extent, jnp.float32)
    if cuts:
        drawn = drawn * level_of(own_key, extent, cuts, -0.22, 0.18)
    return jnp.clip(spiked(drawn, jax.random.fold_in(own_key, 3), *heavy), -reach, reach).astype(dtype)


def setup_inputs(seed: int = 0) -> dict:
    streams_of = jax.random.split(jax.random.key(seed), 5)
    propagation = noise_with(streams_of[0], (N_DEPTH, SLAB, N), (INNER // 8) ** -0.5, 0.21875, ((0, 6), (1, 8), (2, 16)), (0, 2, 2, 2.0))
    tile_mask = draw_tile_mask(jax.random.fold_in(streams_of[4], 71), 0)
    features = gaussian(streams_of[2], (N_DEPTH, SLAB, C), 1.0, 6.0, ((0, 6), (1, 8), (2, 16)))
    teleport = gaussian(streams_of[3], (N, C), 1.0, 6.0, ((0, 768),))
    return dict(propagation=propagation, tile_mask=tile_mask, features=features, teleport=teleport)


def reference(propagation, tile_mask, features, teleport):
    keep = jnp.repeat(jnp.repeat(tile_mask, 128, axis=1), 128, axis=2).astype(jnp.bfloat16)
    masked = propagation * keep
    spread = jnp.zeros((masked.shape[2], features.shape[2]), jnp.float32)
    for slab_index in range(masked.shape[0]):
        spread = spread + lax.dot_general(masked[slab_index], features[slab_index], (((0,), (0,)), ((), ())), preferred_element_type=jnp.float32)
    return 0.9 * spread + 0.1 * teleport.astype(jnp.float32)
```

```python
import functools

import jax
import jax.numpy as jnp
from jax import lax
from jax.experimental import pallas as pl
from jax.experimental.pallas import tpu as pltpu
from jax.sharding import Mesh, PartitionSpec as P

X = 4
Z = 12
ZH = 2
ROWS = 64
SRC = 256
CLS = 256
TGT = Z * ROWS
SEG = TGT // ZH
TILE = 128
STEP = 8.0
TOP = 32000.0


def mask_kernel(mask_ref, a_ref, o_ref):
    i = pl.program_id(0)
    for j in range(ZH * X * SEG // TILE):
        seg, part = divmod(j * TILE, SEG)
        zh, x = divmod(seg, X)
        keep = mask_ref[i, j].astype(jnp.float32)
        tile = a_ref[:, j * TILE : (j + 1) * TILE].astype(jnp.float32) * keep
        o_ref[x, :, zh * SEG + part : zh * SEG + part + TILE] = tile.astype(jnp.bfloat16)


def mask_blocks(mask, a):
    return pl.pallas_call(
        mask_kernel,
        grid=(SRC // TILE,),
        in_specs=[
            pl.BlockSpec(memory_space=pltpu.SMEM),
            pl.BlockSpec((TILE, ZH * X * SEG), lambda i: (i, 0)),
        ],
        out_specs=pl.BlockSpec((X, TILE, TGT), lambda i: (0, i, 0)),
        out_shape=jax.ShapeDtypeStruct((X, SRC, TGT), jnp.bfloat16),
        name="mask_blocks",
    )(mask, a)


def product_kernel(a_ref, f_ref, o_ref):
    total = jnp.zeros((2 * ROWS, CLS), jnp.float32)
    for x in range(X):
        total += lax.dot_general(
            a_ref[x], f_ref[x], (((0,), (1,)), ((), ())), preferred_element_type=jnp.float32
        )
    top = jnp.max(jnp.abs(total), axis=1, keepdims=True)
    power = jnp.ceil(jnp.log2(jnp.maximum(top, 1e-30)) * STEP)
    coded = jnp.round(total * (TOP * jnp.exp2(power * (-1.0 / STEP)))).astype(jnp.int32)
    power = power.astype(jnp.int32)
    lane = lax.broadcasted_iota(jnp.int32, (16, TILE), 1)
    for b in range(2):
        rows = slice(b * ROWS, (b + 1) * ROWS)
        o_ref[b, 0:ROWS, :] = coded[rows, 0:TILE].astype(jnp.int16)
        o_ref[b, ROWS : 2 * ROWS, :] = coded[rows, TILE : 2 * TILE].astype(jnp.int16)
        scales = jnp.zeros((16, TILE), jnp.int32)
        for k in range(4):
            at = b * ROWS + 16 * k
            scales = jnp.where(lane // 32 == k, power[at : at + 16, :], scales)
        o_ref[b, 2 * ROWS : 2 * ROWS + 16, :] = scales.astype(jnp.int16)


def product(blocks, feats):
    return pl.pallas_call(
        product_kernel,
        grid=(Z // 2,),
        in_specs=[
            pl.BlockSpec((X, SRC, 2 * ROWS), lambda i: (0, 0, i)),
            pl.BlockSpec((X, CLS, SRC), lambda i: (0, 0, 0)),
        ],
        out_specs=pl.BlockSpec((2, 2 * ROWS + 16, TILE), lambda i: (i, 0, 0)),
        out_shape=jax.ShapeDtypeStruct((Z, 2 * ROWS + 16, TILE), jnp.int16),
        name="product",
    )(blocks, feats)


def finish_kernel(q_ref, t_ref, o_ref):
    left = jnp.zeros((ROWS, TILE), jnp.float32)
    right = jnp.zeros((ROWS, TILE), jnp.float32)
    for z in range(Z):
        power = q_ref[z, 2 * ROWS : 2 * ROWS + 16, :].astype(jnp.float32)
        scale = jnp.exp2(power * (1.0 / STEP)) * (1.0 / TOP)
        scale = jnp.concatenate([scale[:, 32 * k : 32 * k + 1] for k in range(4)], axis=0)
        left += q_ref[z, 0:ROWS, :].astype(jnp.float32) * scale
        right += q_ref[z, ROWS : 2 * ROWS, :].astype(jnp.float32) * scale
    o_ref[:, 0:TILE] = 0.9 * left + 0.1 * t_ref[:, 0:TILE].astype(jnp.float32)
    o_ref[:, TILE : 2 * TILE] = 0.9 * right + 0.1 * t_ref[:, TILE : 2 * TILE].astype(jnp.float32)


def finish(coded, teleport):
    return pl.pallas_call(
        finish_kernel,
        out_shape=jax.ShapeDtypeStruct((ROWS, CLS), jnp.float32),
        name="finish",
    )(coded, teleport)


def local(propagation, tile_mask, features, teleport):
    blocks = mask_blocks(tile_mask[0], propagation[0])
    blocks = lax.all_to_all(blocks, "x", 0, 0, tiled=True)
    mine = jnp.broadcast_to(features[0].T[None], (X * 16, 16, SRC))
    feats = lax.all_to_all(mine, ("x", "y", "c"), 0, 0, tiled=True).reshape(X, CLS, SRC)
    coded = product(blocks, feats)
    coded = lax.all_to_all(coded, ("zh", "zl"), 0, 0, tiled=True)
    return finish(coded, teleport)


def solution(mesh):
    devices = mesh.devices.reshape(8, 2, ZH, X, 6)
    fine = Mesh(devices, ("y", "c", "zh", "x", "zl"))
    row, col, depth = ("y", "c"), ("zh", "x"), "zl"
    spec = P(depth, col, row)
    return jax.shard_map(
        local,
        mesh=fine,
        in_specs=(spec, spec, spec, P((*row, *col, depth), None)),
        out_specs=P((*row, *col, depth), None),
        check_vma=False,
    )
```

```python
import functools

import jax
import jax.numpy as jnp
from jax import lax
from jax.experimental import pallas as pl
from jax.experimental.pallas import tpu as pltpu
from jax.sharding import Mesh, PartitionSpec as P

X = 4
Y = 8
CORES = 2
Z = 12
ZH = 2
ROWS = 64
SRC = 256
CLS = 256
HELD = CLS // (Y * CORES)
TGT = Z * ROWS
SEG = TGT // ZH
TILE = 128
STEP = 8.0
TOP = 32000.0
MIB = 1 << 20


def mask_kernel(n, me_ref, mask_ref, *refs):
    i = pl.program_id(0)
    for k in range(n):
        for zh in range(ZH):
            a_ref = refs[k * ZH + zh]
            first = (zh * X + lax.rem(me_ref[0] + me_ref[1] + k, X)) * (SEG // TILE)
            for p in range(SEG // TILE):
                keep = mask_ref[i, first + p].astype(jnp.float32)
                tile = a_ref[:, p * TILE : (p + 1) * TILE].astype(jnp.float32) * keep
                to = zh * SEG + p * TILE
                refs[n * ZH + k][:, to : to + TILE] = tile.astype(jnp.bfloat16)


def own_kernel(me_ref, mask_ref, a0_ref, a1_ref, f_ref, o_ref, copies_ref):
    mask_kernel(1, me_ref, mask_ref, a0_ref, a1_ref, o_ref)
    copies_ref[...] = jnp.broadcast_to(f_ref[...][None], copies_ref.shape)


def mask_specs(n, first):
    def segment(k, zh):
        return pl.BlockSpec((TILE, SEG), lambda i, me: (i, zh * X + lax.rem(me[0] + first + k, X)))

    return [pl.BlockSpec(memory_space=pltpu.SMEM)] + [segment(k, zh) for k in range(n) for zh in range(ZH)]


def mask_others(me, mask, a):
    n = X - 1
    return pl.pallas_call(
        functools.partial(mask_kernel, n),
        grid_spec=pltpu.PrefetchScalarGridSpec(
            num_scalar_prefetch=1,
            grid=(SRC // TILE,),
            in_specs=mask_specs(n, 1),
            out_specs=[pl.BlockSpec((TILE, TGT), lambda i, me: (i, 0))] * n,
        ),
        out_shape=[jax.ShapeDtypeStruct((SRC, TGT), jnp.bfloat16)] * n,
        compiler_params=pltpu.CompilerParams(vmem_limit_bytes=16 * MIB),
        name="mask_others",
    )(jnp.stack([me, jnp.int32(1)]), mask, *[a] * (n * ZH))


def mask_own(me, mask, a, feats):
    half = X * Y * TILE // SRC
    return pl.pallas_call(
        own_kernel,
        grid_spec=pltpu.PrefetchScalarGridSpec(
            num_scalar_prefetch=1,
            grid=(SRC // TILE,),
            in_specs=mask_specs(1, 0) + [pl.BlockSpec((HELD, SRC), lambda i, me: (0, 0))],
            out_specs=[
                pl.BlockSpec((TILE, TGT), lambda i, me: (i, 0)),
                pl.BlockSpec((half, HELD, SRC), lambda i, me: (i, 0, 0)),
            ],
        ),
        out_shape=[
            jax.ShapeDtypeStruct((SRC, TGT), jnp.bfloat16),
            jax.ShapeDtypeStruct((X * Y, HELD, SRC), jnp.bfloat16),
        ],
        compiler_params=pltpu.CompilerParams(vmem_limit_bytes=16 * MIB),
        name="mask_own",
    )(jnp.stack([me, jnp.int32(0)]), mask, a, a, feats)


def product_kernel(me_ref, f_ref, *refs):
    o_ref = refs[X]
    feats = []
    for k in range(X):
        x = lax.rem(me_ref[0] + X - k, X)
        feats.append(jnp.concatenate([f_ref[c, x, y] for y in range(Y) for c in range(CORES)], axis=0))
    lane = lax.broadcasted_iota(jnp.int32, (16, TILE), 1)
    wide = 2 * TILE
    for i in range(TGT // wide):
        total = jnp.zeros((CLS, wide), jnp.float32)
        for k in range(X):
            total += jnp.dot(
                feats[k], refs[k][:, i * wide : (i + 1) * wide], preferred_element_type=jnp.float32
            )
        total = total.T
        top = jnp.max(jnp.abs(total), axis=1, keepdims=True)
        power = jnp.ceil(jnp.log2(jnp.maximum(top, 1e-30)) * STEP)
        coded = jnp.round(total * (TOP * jnp.exp2(power * (-1.0 / STEP)))).astype(jnp.int32)
        power = power.astype(jnp.int32)
        for b in range(wide // ROWS):
            z = i * (wide // ROWS) + b
            rows = slice(b * ROWS, (b + 1) * ROWS)
            o_ref[z, 0:ROWS, :] = coded[rows, 0:TILE].astype(jnp.int16)
            o_ref[z, ROWS : 2 * ROWS, :] = coded[rows, TILE : 2 * TILE].astype(jnp.int16)
            scales = jnp.zeros((16, TILE), jnp.int32)
            for k in range(4):
                at = b * ROWS + 16 * k
                scales = jnp.where(lane // 32 == k, power[at : at + 16, :], scales)
            o_ref[z, 2 * ROWS : 2 * ROWS + 16, :] = scales.astype(jnp.int16)


def product(me, feats, blocks):
    whole = pl.BlockSpec(memory_space=pltpu.VMEM)
    return pl.pallas_call(
        product_kernel,
        in_specs=[pl.BlockSpec(memory_space=pltpu.SMEM)] + [whole] * (1 + X),
        out_specs=whole,
        out_shape=jax.ShapeDtypeStruct((Z, 2 * ROWS + 16, TILE), jnp.int16),
        compiler_params=pltpu.CompilerParams(vmem_limit_bytes=16 * MIB),
        name="product",
    )(me, feats, *blocks)


def finish_kernel(q_ref, t_ref, o_ref):
    left = jnp.zeros((ROWS, TILE), jnp.float32)
    right = jnp.zeros((ROWS, TILE), jnp.float32)
    for z in range(Z):
        power = q_ref[z, 2 * ROWS : 2 * ROWS + 16, :].astype(jnp.float32)
        scale = jnp.exp2(power * (1.0 / STEP)) * (1.0 / TOP)
        scale = jnp.concatenate([scale[:, 32 * k : 32 * k + 1] for k in range(4)], axis=0)
        left += q_ref[z, 0:ROWS, :].astype(jnp.float32) * scale
        right += q_ref[z, ROWS : 2 * ROWS, :].astype(jnp.float32) * scale
    o_ref[:, 0:TILE] = 0.9 * left + 0.1 * t_ref[:, 0:TILE].astype(jnp.float32)
    o_ref[:, TILE : 2 * TILE] = 0.9 * right + 0.1 * t_ref[:, TILE : 2 * TILE].astype(jnp.float32)


def finish(coded, teleport):
    return pl.pallas_call(
        finish_kernel,
        out_shape=jax.ShapeDtypeStruct((ROWS, CLS), jnp.float32),
        compiler_params=pltpu.CompilerParams(vmem_limit_bytes=16 * MIB),
        name="finish",
    )(coded, teleport)


def local(propagation, tile_mask, features, teleport):
    me = lax.axis_index("x").astype(jnp.int32)
    others = mask_others(me, tile_mask[0], propagation[0])
    blocks = [lax.ppermute(b, "x", [(i, (i + k) % X) for i in range(X)]) for k, b in enumerate(others, 1)]
    mine = lax.optimization_barrier((features[0].T, *others))[0]
    own, copies = mask_own(me, tile_mask[0], propagation[0], mine)
    copies, blocks[0] = lax.optimization_barrier((copies, blocks[0]))
    feats = lax.all_to_all(copies, ("x", "y"), 0, 0, tiled=True)
    feats = lax.all_gather(feats, "c", axis=0).reshape(CORES, X, Y, HELD, SRC)
    coded = product(me[None], feats, [own, *blocks])
    coded = lax.all_to_all(coded, ("zh", "zl"), 0, 0, tiled=True)
    return finish(coded, teleport)


def solution(mesh):
    devices = mesh.devices.reshape(Y, CORES, ZH, X, Z // ZH)
    fine = Mesh(devices, ("y", "c", "zh", "x", "zl"))
    row, col, depth = ("y", "c"), ("zh", "x"), "zl"
    spec = P(depth, col, row)
    return jax.shard_map(
        local,
        mesh=fine,
        in_specs=(spec, spec, spec, P((*row, *col, depth), None)),
        out_specs=P((*row, *col, depth), None),
        check_vma=False,
    )
```

```python
import functools

import jax
import jax.numpy as jnp
from jax import lax
from jax.experimental import pallas as pl
from jax.experimental.pallas import tpu as pltpu
from jax.sharding import Mesh, PartitionSpec as P

X = 4
Y = 8
CORES = 2
Z = 12
ZH = 2
ROWS = 64
SRC = 256
CLS = 256
HELD = CLS // (Y * CORES)
TGT = Z * ROWS
SEG = TGT // ZH
TILE = 128
STEP = 8.0
TOP = 32000.0
MIB = 1 << 20


def mask_kernel(n, me_ref, mask_ref, *refs):
    i = pl.program_id(0)
    for k in range(n):
        for zh in range(ZH):
            a_ref = refs[k * ZH + zh]
            first = (zh * X + lax.rem(me_ref[0] + me_ref[1] + k, X)) * (SEG // TILE)
            for p in range(SEG // TILE):
                keep = mask_ref[i, first + p].astype(jnp.float32)
                tile = a_ref[:, p * TILE : (p + 1) * TILE].astype(jnp.float32) * keep
                to = zh * SEG + p * TILE
                refs[n * ZH + k][:, to : to + TILE] = tile.astype(jnp.bfloat16)


def own_kernel(me_ref, mask_ref, a0_ref, a1_ref, f_ref, o_ref, copies_ref):
    mask_kernel(1, me_ref, mask_ref, a0_ref, a1_ref, o_ref)
    copies_ref[...] = jnp.broadcast_to(f_ref[...][None], copies_ref.shape)


def mask_specs(n, first):
    def segment(k, zh):
        return pl.BlockSpec((TILE, SEG), lambda i, me: (i, zh * X + lax.rem(me[0] + first + k, X)))

    return [pl.BlockSpec(memory_space=pltpu.SMEM)] + [segment(k, zh) for k in range(n) for zh in range(ZH)]


def mask_others(me, mask, a):
    n = X - 1
    return pl.pallas_call(
        functools.partial(mask_kernel, n),
        grid_spec=pltpu.PrefetchScalarGridSpec(
            num_scalar_prefetch=1,
            grid=(SRC // TILE,),
            in_specs=mask_specs(n, 1),
            out_specs=[pl.BlockSpec((TILE, TGT), lambda i, me: (i, 0))] * n,
        ),
        out_shape=[jax.ShapeDtypeStruct((SRC, TGT), jnp.bfloat16)] * n,
        compiler_params=pltpu.CompilerParams(vmem_limit_bytes=16 * MIB),
        name="mask_others",
    )(jnp.stack([me, jnp.int32(1)]), mask, *[a] * (n * ZH))


def mask_own(me, mask, a, feats):
    half = X * Y * TILE // SRC
    return pl.pallas_call(
        own_kernel,
        grid_spec=pltpu.PrefetchScalarGridSpec(
            num_scalar_prefetch=1,
            grid=(SRC // TILE,),
            in_specs=mask_specs(1, 0) + [pl.BlockSpec((HELD, SRC), lambda i, me: (0, 0))],
            out_specs=[
                pl.BlockSpec((TILE, TGT), lambda i, me: (i, 0)),
                pl.BlockSpec((half, HELD, SRC), lambda i, me: (i, 0, 0)),
            ],
        ),
        out_shape=[
            jax.ShapeDtypeStruct((SRC, TGT), jnp.bfloat16),
            jax.ShapeDtypeStruct((X * Y, HELD, SRC), jnp.bfloat16),
        ],
        compiler_params=pltpu.CompilerParams(vmem_limit_bytes=16 * MIB),
        name="mask_own",
    )(jnp.stack([me, jnp.int32(0)]), mask, a, a, feats)


def product_kernel(me_ref, f_ref, *refs):
    o_ref = refs[X]
    feats = []
    for k in range(X):
        x = lax.rem(me_ref[0] + X - k, X)
        feats.append(jnp.concatenate([f_ref[c, x, y] for y in range(Y) for c in range(CORES)], axis=0))
    lane = lax.broadcasted_iota(jnp.int32, (16, TILE), 1)
    wide = 2 * TILE
    for i in range(TGT // wide):
        total = jnp.zeros((CLS, wide), jnp.float32)
        for k in range(X):
            total += jnp.dot(
                feats[k], refs[k][:, i * wide : (i + 1) * wide], preferred_element_type=jnp.float32
            )
        total = total.T
        top = jnp.max(jnp.abs(total), axis=1, keepdims=True)
        power = jnp.ceil(jnp.log2(jnp.maximum(top, 1e-30)) * STEP)
        coded = jnp.round(total * (TOP * jnp.exp2(power * (-1.0 / STEP)))).astype(jnp.int32)
        power = power.astype(jnp.int32)
        for b in range(wide // ROWS):
            z = i * (wide // ROWS) + b
            rows = slice(b * ROWS, (b + 1) * ROWS)
            o_ref[z, 0:ROWS, :] = coded[rows, 0:TILE].astype(jnp.int16)
            o_ref[z, ROWS : 2 * ROWS, :] = coded[rows, TILE : 2 * TILE].astype(jnp.int16)
            scales = jnp.zeros((16, TILE), jnp.int32)
            for k in range(4):
                at = b * ROWS + 16 * k
                scales = jnp.where(lane // 32 == k, power[at : at + 16, :], scales)
            o_ref[z, 2 * ROWS : 2 * ROWS + 16, :] = scales.astype(jnp.int16)


def product(me, feats, blocks):
    whole = pl.BlockSpec(memory_space=pltpu.VMEM)
    return pl.pallas_call(
        product_kernel,
        in_specs=[pl.BlockSpec(memory_space=pltpu.SMEM)] + [whole] * (1 + X),
        out_specs=whole,
        out_shape=jax.ShapeDtypeStruct((Z, 2 * ROWS + 16, TILE), jnp.int16),
        compiler_params=pltpu.CompilerParams(vmem_limit_bytes=16 * MIB),
        name="product",
    )(me, feats, *blocks)


def finish_kernel(q_ref, t_ref, o_ref):
    left = jnp.zeros((ROWS, TILE), jnp.float32)
    right = jnp.zeros((ROWS, TILE), jnp.float32)
    for z in range(Z):
        power = q_ref[z, 2 * ROWS : 2 * ROWS + 16, :].astype(jnp.float32)
        scale = jnp.exp2(power * (1.0 / STEP)) * (1.0 / TOP)
        scale = jnp.concatenate([scale[:, 32 * k : 32 * k + 1] for k in range(4)], axis=0)
        left += q_ref[z, 0:ROWS, :].astype(jnp.float32) * scale
        right += q_ref[z, ROWS : 2 * ROWS, :].astype(jnp.float32) * scale
    o_ref[:, 0:TILE] = 0.9 * left + 0.1 * t_ref[:, 0:TILE].astype(jnp.float32)
    o_ref[:, TILE : 2 * TILE] = 0.9 * right + 0.1 * t_ref[:, TILE : 2 * TILE].astype(jnp.float32)


def finish(coded, teleport):
    return pl.pallas_call(
        finish_kernel,
        out_shape=jax.ShapeDtypeStruct((ROWS, CLS), jnp.float32),
        compiler_params=pltpu.CompilerParams(vmem_limit_bytes=16 * MIB),
        name="finish",
    )(coded, teleport)


def local(propagation, tile_mask, features, teleport):
    me = lax.axis_index("x").astype(jnp.int32)
    others = mask_others(me, tile_mask[0], propagation[0])
    blocks = [lax.ppermute(b, "x", [(i, (i + k) % X) for i in range(X)]) for k, b in enumerate(others, 1)]
    mine = lax.optimization_barrier((features[0].T, *others))[0]
    own, copies = mask_own(me, tile_mask[0], propagation[0], mine)
    feats = lax.cond(
        me < X,
        lambda c: lax.all_gather(lax.all_to_all(c, ("x", "y"), 0, 0, tiled=True), "c", axis=0),
        lambda c: jnp.stack([c] * CORES),
        copies,
    ).reshape(CORES, X, Y, HELD, SRC)
    coded = product(me[None], feats, [own, *blocks])
    coded = lax.all_to_all(coded, ("zh", "zl"), 0, 0, tiled=True)
    return finish(coded, teleport)


def solution(mesh):
    devices = mesh.devices.reshape(Y, CORES, ZH, X, Z // ZH)
    fine = Mesh(devices, ("y", "c", "zh", "x", "zl"))
    row, col, depth = ("y", "c"), ("zh", "x"), "zl"
    spec = P(depth, col, row)
    return jax.shard_map(
        local,
        mesh=fine,
        in_specs=(spec, spec, spec, P((*row, *col, depth), None)),
        out_specs=P((*row, *col, depth), None),
        check_vma=False,
    )
```

```python
import functools

import jax
import jax.numpy as jnp
from jax import lax
from jax.experimental import pallas as pl
from jax.experimental.pallas import tpu as pltpu
from jax.sharding import Mesh, PartitionSpec as P

X = 4
Y = 8
CORES = 2
Z = 12
ZH = 2
ROWS = 64
SRC = 256
CLS = 256
HELD = CLS // (Y * CORES)
TGT = Z * ROWS
SEG = TGT // ZH
TILE = 128
STEP = 8.0
TOP = 32000.0
MIB = 1 << 20
LIMIT = 60


def mask_kernel(steps, mask_hbm, a_hbm, *refs):
    n = len(steps)
    o_refs, (mask_ref, a_ref, sems) = refs[:n], refs[-3:]
    me = lax.axis_index("x")
    mask_copy = pltpu.make_async_copy(mask_hbm, mask_ref, sems.at[0])
    mask_copy.start()
    copies = []
    for b, (k, zh) in enumerate((k, zh) for k in steps for zh in range(ZH)):
        first = (zh * X + lax.rem(me + k, X)) * (SEG // TILE)
        columns = pl.ds(pl.multiple_of(first * TILE, TILE), SEG)
        copy = pltpu.make_async_copy(a_hbm.at[:, columns], a_ref.at[b], sems.at[1 + b])
        copy.start()
        copies.append((b, zh, first, copy))
    mask_copy.wait()
    for b, zh, first, copy in copies:
        copy.wait()
        for i in range(SRC // TILE):
            rows = slice(i * TILE, (i + 1) * TILE)
            for p in range(SEG // TILE):
                keep = mask_ref[i, first + p].astype(jnp.float32)
                tile = a_ref[b, rows, p * TILE : (p + 1) * TILE].astype(jnp.float32) * keep
                to = zh * SEG + p * TILE
                o_refs[b // ZH][rows, to : to + TILE] = tile.astype(jnp.bfloat16)


def spread_kernel(steps, mask_hbm, a_hbm, f_ref, *refs):
    n = len(steps)
    refs[n][...] = jnp.broadcast_to(f_ref[...][None], refs[n].shape)
    mask_kernel(steps, mask_hbm, a_hbm, *refs[:n], *refs[n + 1 :])


def mask_blocks(steps, mask, a, feats=None):
    n = len(steps)
    whole = pl.BlockSpec(memory_space=pltpu.VMEM)
    more = [] if feats is None else [feats]
    return pl.pallas_call(
        functools.partial(spread_kernel if more else mask_kernel, steps),
        in_specs=[pl.BlockSpec(memory_space=pl.ANY)] * 2 + [whole] * len(more),
        out_specs=[whole] * (n + len(more)),
        out_shape=[jax.ShapeDtypeStruct((SRC, TGT), jnp.bfloat16)] * n
        + [jax.ShapeDtypeStruct((X * Y, HELD, SRC), jnp.bfloat16)] * len(more),
        scratch_shapes=[
            pltpu.SMEM(mask.shape, jnp.int32),
            pltpu.VMEM((n * ZH, SRC, SEG), jnp.bfloat16),
            pltpu.SemaphoreType.DMA((1 + n * ZH,)),
        ],
        compiler_params=pltpu.CompilerParams(vmem_limit_bytes=LIMIT * MIB),
        name="mask_blocks",
    )(mask, a, *more)


def product_kernel(me_ref, f_ref, *refs):
    o_ref = refs[X]
    feats = []
    for k in range(X):
        x = lax.rem(me_ref[0] + X - k, X)
        feats.append(jnp.concatenate([f_ref[c, x, y] for y in range(Y) for c in range(CORES)], axis=0))
    lane = lax.broadcasted_iota(jnp.int32, (16, TILE), 1)
    wide = 2 * TILE
    for i in range(TGT // wide):
        total = jnp.zeros((CLS, wide), jnp.float32)
        for k in range(X):
            total += jnp.dot(
                feats[k], refs[k][:, i * wide : (i + 1) * wide], preferred_element_type=jnp.float32
            )
        total = total.T
        top = jnp.max(jnp.abs(total), axis=1, keepdims=True)
        power = jnp.ceil(jnp.log2(jnp.maximum(top, 1e-30)) * STEP)
        coded = jnp.round(total * (TOP * jnp.exp2(power * (-1.0 / STEP)))).astype(jnp.int32)
        power = power.astype(jnp.int32)
        for b in range(wide // ROWS):
            z = i * (wide // ROWS) + b
            rows = slice(b * ROWS, (b + 1) * ROWS)
            o_ref[z, 0:ROWS, :] = coded[rows, 0:TILE].astype(jnp.int16)
            o_ref[z, ROWS : 2 * ROWS, :] = coded[rows, TILE : 2 * TILE].astype(jnp.int16)
            scales = jnp.zeros((16, TILE), jnp.int32)
            for k in range(4):
                at = b * ROWS + 16 * k
                scales = jnp.where(lane // 32 == k, power[at : at + 16, :], scales)
            o_ref[z, 2 * ROWS : 2 * ROWS + 16, :] = scales.astype(jnp.int16)


def product(me, feats, blocks):
    whole = pl.BlockSpec(memory_space=pltpu.VMEM)
    return pl.pallas_call(
        product_kernel,
        in_specs=[pl.BlockSpec(memory_space=pltpu.SMEM)] + [whole] * (1 + X),
        out_specs=whole,
        out_shape=jax.ShapeDtypeStruct((Z, 2 * ROWS + 16, TILE), jnp.int16),
        compiler_params=pltpu.CompilerParams(vmem_limit_bytes=16 * MIB),
        name="product",
    )(me, feats, *blocks)


def finish_kernel(q_ref, t_ref, o_ref):
    left = jnp.zeros((ROWS, TILE), jnp.float32)
    right = jnp.zeros((ROWS, TILE), jnp.float32)
    for z in range(Z):
        power = q_ref[z, 2 * ROWS : 2 * ROWS + 16, :].astype(jnp.float32)
        scale = jnp.exp2(power * (1.0 / STEP)) * (1.0 / TOP)
        scale = jnp.concatenate([scale[:, 32 * k : 32 * k + 1] for k in range(4)], axis=0)
        left += q_ref[z, 0:ROWS, :].astype(jnp.float32) * scale
        right += q_ref[z, ROWS : 2 * ROWS, :].astype(jnp.float32) * scale
    o_ref[:, 0:TILE] = 0.9 * left + 0.1 * t_ref[:, 0:TILE].astype(jnp.float32)
    o_ref[:, TILE : 2 * TILE] = 0.9 * right + 0.1 * t_ref[:, TILE : 2 * TILE].astype(jnp.float32)


def finish(coded, teleport):
    return pl.pallas_call(
        finish_kernel,
        out_shape=jax.ShapeDtypeStruct((ROWS, CLS), jnp.float32),
        compiler_params=pltpu.CompilerParams(vmem_limit_bytes=16 * MIB),
        name="finish",
    )(coded, teleport)


def gather(copies):
    return lax.all_gather(lax.all_to_all(copies, ("x", "y"), 0, 0, tiled=True), "c", axis=0)


def shift(block, k):
    return lax.ppermute(block, "x", [(i, (i + k) % X) for i in range(X)])


def local(propagation, tile_mask, features, teleport):
    mask, a, feats = tile_mask[0], propagation[0], features[0].T
    (far,) = mask_blocks((2,), mask, a)
    up, down, own, copies = mask_blocks((1, 3, 0), mask, a, lax.optimization_barrier((feats, far))[0])
    blocks = [own, shift(up, 1), shift(far, 2), shift(down, 3)]
    me = lax.axis_index("x").astype(jnp.int32)
    feats = lax.cond(me < X, gather, lambda c: jnp.stack([c] * CORES), copies)
    coded = product(me[None], feats.reshape(CORES, X, Y, HELD, SRC), blocks)
    coded = lax.all_to_all(coded, ("zh", "zl"), 0, 0, tiled=True)
    return finish(coded, teleport)


def solution(mesh):
    devices = mesh.devices.reshape(Y, CORES, ZH, X, Z // ZH)
    fine = Mesh(devices, ("y", "c", "zh", "x", "zl"))
    row, col, depth = ("y", "c"), ("zh", "x"), "zl"
    spec = P(depth, col, row)
    return jax.shard_map(
        local,
        mesh=fine,
        in_specs=(spec, spec, spec, P((*row, *col, depth), None)),
        out_specs=P((*row, *col, depth), None),
        check_vma=False,
    )
```

```python
import functools

import jax
import jax.numpy as jnp
from jax import lax
from jax.experimental import pallas as pl
from jax.experimental.pallas import tpu as pltpu
from jax.sharding import Mesh, PartitionSpec as P

X = 4
Y = 8
CORES = 2
Z = 12
ZH = 2
ROWS = 64
SRC = 256
CLS = 256
HELD = CLS // (Y * CORES)
TGT = Z * ROWS
SEG = TGT // ZH
TILE = 128
STEP = 8.0
TOP = 32000.0
MIB = 1 << 20


def mask_kernel(steps, mask_hbm, a_hbm, *refs):
    n = len(steps)
    o_refs, (mask_ref, a_ref, sems) = refs[:n], refs[-3:]
    me = lax.axis_index("x")
    mask_copy = pltpu.make_async_copy(mask_hbm, mask_ref, sems.at[0])
    mask_copy.start()
    copies = []
    for b, (k, zh) in enumerate((k, zh) for k in steps for zh in range(ZH)):
        first = (zh * X + lax.rem(me + k, X)) * (SEG // TILE)
        columns = pl.ds(pl.multiple_of(first * TILE, TILE), SEG)
        copy = pltpu.make_async_copy(a_hbm.at[:, columns], a_ref.at[b], sems.at[1 + b])
        copy.start()
        copies.append((b, zh, first, copy))
    mask_copy.wait()
    for b, zh, first, copy in copies:
        copy.wait()
        for i in range(SRC // TILE):
            rows = slice(i * TILE, (i + 1) * TILE)
            for p in range(SEG // TILE):
                tile = a_ref[b, rows, p * TILE : (p + 1) * TILE]
                to = zh * SEG + p * TILE
                o_refs[b // ZH][rows, to : to + TILE] = jnp.where(mask_ref[i, first + p] != 0, tile, 0)


def spread_kernel(steps, mask_hbm, a_hbm, f_ref, *refs):
    n = len(steps)
    refs[n][...] = jnp.broadcast_to(f_ref[...][None], refs[n].shape)
    mask_kernel(steps, mask_hbm, a_hbm, *refs[:n], *refs[n + 1 :])


def mask_blocks(steps, mask, a, feats=None, limit=60):
    n = len(steps)
    whole = pl.BlockSpec(memory_space=pltpu.VMEM)
    more = [] if feats is None else [feats]
    return pl.pallas_call(
        functools.partial(spread_kernel if more else mask_kernel, steps),
        in_specs=[pl.BlockSpec(memory_space=pl.ANY)] * 2 + [whole] * len(more),
        out_specs=[whole] * (n + len(more)),
        out_shape=[jax.ShapeDtypeStruct((SRC, TGT), jnp.bfloat16)] * n
        + [jax.ShapeDtypeStruct((X * Y, HELD, SRC), jnp.bfloat16)] * len(more),
        scratch_shapes=[
            pltpu.SMEM(mask.shape, jnp.int32),
            pltpu.VMEM((n * ZH, SRC, SEG), jnp.bfloat16),
            pltpu.SemaphoreType.DMA((1 + n * ZH,)),
        ],
        compiler_params=pltpu.CompilerParams(vmem_limit_bytes=limit * MIB),
        name="mask_blocks",
    )(mask, a, *more)


def product_kernel(me_ref, f_ref, *refs):
    o_ref = refs[X]
    feats = []
    for k in range(X):
        x = lax.rem(me_ref[0] + X - k, X)
        feats.append(jnp.concatenate([f_ref[c, x, y] for y in range(Y) for c in range(CORES)], axis=0))
    lane = lax.broadcasted_iota(jnp.int32, (16, TILE), 1)
    wide = 2 * TILE
    for i in range(TGT // wide):
        total = jnp.zeros((CLS, wide), jnp.float32)
        for k in range(X):
            total += jnp.dot(
                feats[k], refs[k][:, i * wide : (i + 1) * wide], preferred_element_type=jnp.float32
            )
        total = total.T
        top = jnp.max(jnp.abs(total), axis=1, keepdims=True)
        power = jnp.ceil(jnp.log2(jnp.maximum(top, 1e-30)) * STEP)
        coded = jnp.round(total * (TOP * jnp.exp2(power * (-1.0 / STEP)))).astype(jnp.int32)
        power = power.astype(jnp.int32)
        for b in range(wide // ROWS):
            z = i * (wide // ROWS) + b
            rows = slice(b * ROWS, (b + 1) * ROWS)
            o_ref[z, 0:ROWS, :] = coded[rows, 0:TILE].astype(jnp.int16)
            o_ref[z, ROWS : 2 * ROWS, :] = coded[rows, TILE : 2 * TILE].astype(jnp.int16)
            scales = jnp.zeros((16, TILE), jnp.int32)
            for k in range(4):
                at = b * ROWS + 16 * k
                scales = jnp.where(lane // 32 == k, power[at : at + 16, :], scales)
            o_ref[z, 2 * ROWS : 2 * ROWS + 16, :] = scales.astype(jnp.int16)


def product(me, feats, blocks):
    whole = pl.BlockSpec(memory_space=pltpu.VMEM)
    return pl.pallas_call(
        product_kernel,
        in_specs=[pl.BlockSpec(memory_space=pltpu.SMEM)] + [whole] * (1 + X),
        out_specs=whole,
        out_shape=jax.ShapeDtypeStruct((Z, 2 * ROWS + 16, TILE), jnp.int16),
        compiler_params=pltpu.CompilerParams(vmem_limit_bytes=16 * MIB),
        name="product",
    )(me, feats, *blocks)


def finish_kernel(q_ref, t_ref, o_ref):
    left = jnp.zeros((ROWS, TILE), jnp.float32)
    right = jnp.zeros((ROWS, TILE), jnp.float32)
    for z in range(Z):
        power = q_ref[z, 2 * ROWS : 2 * ROWS + 16, :].astype(jnp.float32)
        scale = jnp.exp2(power * (1.0 / STEP)) * (1.0 / TOP)
        scale = jnp.concatenate([scale[:, 32 * k : 32 * k + 1] for k in range(4)], axis=0)
        left += q_ref[z, 0:ROWS, :].astype(jnp.float32) * scale
        right += q_ref[z, ROWS : 2 * ROWS, :].astype(jnp.float32) * scale
    o_ref[:, 0:TILE] = 0.9 * left + 0.1 * t_ref[:, 0:TILE].astype(jnp.float32)
    o_ref[:, TILE : 2 * TILE] = 0.9 * right + 0.1 * t_ref[:, TILE : 2 * TILE].astype(jnp.float32)


def finish(coded, teleport):
    return pl.pallas_call(
        finish_kernel,
        out_shape=jax.ShapeDtypeStruct((ROWS, CLS), jnp.float32),
        compiler_params=pltpu.CompilerParams(vmem_limit_bytes=16 * MIB),
        name="finish",
    )(coded, teleport)


def shift(block, k):
    return lax.ppermute(block, "x", [(i, (i + k) % X) for i in range(X)])


def local(propagation, tile_mask, features, teleport):
    mask, a = tile_mask[0], propagation[0]
    far, copies = mask_blocks((2,), mask, a, features[0].T)
    feats = lax.all_to_all(copies, ("x", "y"), 0, 0, tiled=True)
    feats = lax.all_gather(feats, "c", axis=0).reshape(CORES, X, Y, HELD, SRC)
    near_a, _ = lax.optimization_barrier((a, far))
    up, down = mask_blocks((1, 3), mask, near_a, limit=16)
    own_a, _ = lax.optimization_barrier((a, up))
    (own,) = mask_blocks((0,), mask, own_a, limit=16)
    blocks = [own, shift(up, 1), shift(far, 2), shift(down, 3)]
    me = lax.axis_index("x").astype(jnp.int32)
    coded = product(me[None], feats, blocks)
    coded = lax.all_to_all(coded, ("zh", "zl"), 0, 0, tiled=True)
    return finish(coded, teleport)


def solution(mesh):
    devices = mesh.devices.reshape(Y, CORES, ZH, X, Z // ZH)
    fine = Mesh(devices, ("y", "c", "zh", "x", "zl"))
    row, col, depth = ("y", "c"), ("zh", "x"), "zl"
    spec = P(depth, col, row)
    return jax.shard_map(
        local,
        mesh=fine,
        in_specs=(spec, spec, spec, P((*row, *col, depth), None)),
        out_specs=P((*row, *col, depth), None),
        check_vma=False,
    )
```

```python
import functools

import jax
import jax.numpy as jnp
from jax import lax
from jax.experimental import pallas as pl
from jax.experimental.pallas import tpu as pltpu
from jax.sharding import Mesh, PartitionSpec as P

X = 4
Y = 8
CORES = 2
Z = 12
ZH = 2
ROWS = 64
SRC = 256
CLS = 256
HELD = CLS // (Y * CORES)
TGT = Z * ROWS
SEG = TGT // ZH
TILE = 128
STEP = 8.0
TOP = 32000.0
MIB = 1 << 20


def mask_kernel(steps, mask_hbm, a_hbm, *refs):
    n = len(steps)
    o_refs, (mask_ref, a_ref, sems) = refs[:n], refs[-3:]
    me = lax.axis_index("x")
    mask_copy = pltpu.make_async_copy(mask_hbm, mask_ref, sems.at[0])
    mask_copy.start()
    copies = []
    for b, (k, zh) in enumerate((k, zh) for k in steps for zh in range(ZH)):
        first = (zh * X + lax.rem(me + k, X)) * (SEG // TILE)
        columns = pl.ds(pl.multiple_of(first * TILE, TILE), SEG)
        copy = pltpu.make_async_copy(a_hbm.at[:, columns], a_ref.at[b], sems.at[1 + b])
        copy.start()
        copies.append((b, zh, first, copy))
    mask_copy.wait()
    for b, zh, first, copy in copies:
        copy.wait()
        for i in range(SRC // TILE):
            rows = slice(i * TILE, (i + 1) * TILE)
            for p in range(SEG // TILE):
                tile = a_ref[b, rows, p * TILE : (p + 1) * TILE]
                to = zh * SEG + p * TILE
                o_refs[b // ZH][rows, to : to + TILE] = jnp.where(mask_ref[i, first + p] != 0, tile, 0)


def spread_kernel(steps, mask_hbm, a_hbm, f_ref, *refs):
    n = len(steps)
    refs[n][...] = jnp.broadcast_to(f_ref[...][None], refs[n].shape)
    mask_kernel(steps, mask_hbm, a_hbm, *refs[:n], *refs[n + 1 :])


def mask_blocks(steps, mask, a, feats=None, limit=60):
    n = len(steps)
    whole = pl.BlockSpec(memory_space=pltpu.VMEM)
    more = [] if feats is None else [feats]
    return pl.pallas_call(
        functools.partial(spread_kernel if more else mask_kernel, steps),
        in_specs=[pl.BlockSpec(memory_space=pl.ANY)] * 2 + [whole] * len(more),
        out_specs=[whole] * (n + len(more)),
        out_shape=[jax.ShapeDtypeStruct((SRC, TGT), jnp.bfloat16)] * n
        + [jax.ShapeDtypeStruct((X * Y, HELD, SRC), jnp.bfloat16)] * len(more),
        scratch_shapes=[
            pltpu.SMEM(mask.shape, jnp.int32),
            pltpu.VMEM((n * ZH, SRC, SEG), jnp.bfloat16),
            pltpu.SemaphoreType.DMA((1 + n * ZH,)),
        ],
        compiler_params=pltpu.CompilerParams(vmem_limit_bytes=limit * MIB),
        name="mask_blocks",
    )(mask, a, *more)


def product_kernel(me_ref, f_ref, *refs):
    o_ref = refs[X]
    feats = []
    for k in range(X):
        x = lax.rem(me_ref[0] + X - k, X)
        feats.append(jnp.concatenate([f_ref[c, x, y] for y in range(Y) for c in range(CORES)], axis=0))
    lane = lax.broadcasted_iota(jnp.int32, (16, TILE), 1)
    wide = 2 * TILE
    for i in range(TGT // wide):
        total = jnp.zeros((CLS, wide), jnp.float32)
        for k in range(X):
            total += jnp.dot(
                feats[k], refs[k][:, i * wide : (i + 1) * wide], preferred_element_type=jnp.float32
            )
        total = total.T
        top = jnp.max(jnp.abs(total), axis=1, keepdims=True)
        power = jnp.ceil(jnp.log2(jnp.maximum(top, 1e-30)) * STEP)
        coded = jnp.round(total * (TOP * jnp.exp2(power * (-1.0 / STEP)))).astype(jnp.int32)
        power = power.astype(jnp.int32)
        for b in range(wide // ROWS):
            z = i * (wide // ROWS) + b
            rows = slice(b * ROWS, (b + 1) * ROWS)
            o_ref[z, 0:ROWS, :] = coded[rows, 0:TILE].astype(jnp.int16)
            o_ref[z, ROWS : 2 * ROWS, :] = coded[rows, TILE : 2 * TILE].astype(jnp.int16)
            scales = jnp.zeros((16, TILE), jnp.int32)
            for k in range(4):
                at = b * ROWS + 16 * k
                scales = jnp.where(lane // 32 == k, power[at : at + 16, :], scales)
            o_ref[z, 2 * ROWS : 2 * ROWS + 16, :] = scales.astype(jnp.int16)


def product(me, feats, blocks):
    whole = pl.BlockSpec(memory_space=pltpu.VMEM)
    return pl.pallas_call(
        product_kernel,
        in_specs=[pl.BlockSpec(memory_space=pltpu.SMEM)] + [whole] * (1 + X),
        out_specs=whole,
        out_shape=jax.ShapeDtypeStruct((Z, 2 * ROWS + 16, TILE), jnp.int16),
        compiler_params=pltpu.CompilerParams(vmem_limit_bytes=16 * MIB),
        name="product",
    )(me, feats, *blocks)


def finish_kernel(q_ref, t_ref, o_ref):
    left = jnp.zeros((ROWS, TILE), jnp.float32)
    right = jnp.zeros((ROWS, TILE), jnp.float32)
    for z in range(Z):
        power = q_ref[z, 2 * ROWS : 2 * ROWS + 16, :].astype(jnp.float32)
        scale = jnp.exp2(power * (1.0 / STEP)) * (1.0 / TOP)
        scale = jnp.concatenate([scale[:, 32 * k : 32 * k + 1] for k in range(4)], axis=0)
        left += q_ref[z, 0:ROWS, :].astype(jnp.float32) * scale
        right += q_ref[z, ROWS : 2 * ROWS, :].astype(jnp.float32) * scale
    o_ref[:, 0:TILE] = 0.9 * left + 0.1 * t_ref[:, 0:TILE].astype(jnp.float32)
    o_ref[:, TILE : 2 * TILE] = 0.9 * right + 0.1 * t_ref[:, TILE : 2 * TILE].astype(jnp.float32)


def finish(coded, teleport):
    return pl.pallas_call(
        finish_kernel,
        out_shape=jax.ShapeDtypeStruct((ROWS, CLS), jnp.float32),
        compiler_params=pltpu.CompilerParams(vmem_limit_bytes=16 * MIB),
        name="finish",
    )(coded, teleport)


def shift(block, k):
    return lax.ppermute(block, "x", [(i, (i + k) % X) for i in range(X)])


def others(operands):
    mask, a, feats = operands
    copies = jnp.broadcast_to(feats[None], (X * Y, HELD, SRC))
    feats = lax.all_to_all(copies, ("x", "y"), 0, 0, tiled=True)
    feats = lax.all_gather(feats, "c", axis=0)
    up, down = mask_blocks((1, 3), mask, a, limit=16)
    own_a, _ = lax.optimization_barrier((a, up))
    (own,) = mask_blocks((0,), mask, own_a, limit=16)
    return feats, own, shift(up, 1), shift(down, 3)


def nothing(operands):
    block = jnp.zeros((SRC, TGT), jnp.bfloat16)
    return jnp.zeros((CORES, X * Y, HELD, SRC), jnp.bfloat16), block, block, block


def local(propagation, tile_mask, features, teleport):
    mask, a = tile_mask[0], propagation[0]
    (far,) = mask_blocks((2,), mask, a)
    me = lax.axis_index("x").astype(jnp.int32)
    a, _ = lax.optimization_barrier((a, far))
    feats, own, up, down = lax.cond(me < X, others, nothing, (mask, a, features[0].T))
    feats = feats.reshape(CORES, X, Y, HELD, SRC)
    coded = product(me[None], feats, [own, up, shift(far, 2), down])
    coded = lax.all_to_all(coded, ("zh", "zl"), 0, 0, tiled=True)
    return finish(coded, teleport)


def solution(mesh):
    devices = mesh.devices.reshape(Y, CORES, ZH, X, Z // ZH)
    fine = Mesh(devices, ("y", "c", "zh", "x", "zl"))
    row, col, depth = ("y", "c"), ("zh", "x"), "zl"
    spec = P(depth, col, row)
    return jax.shard_map(
        local,
        mesh=fine,
        in_specs=(spec, spec, spec, P((*row, *col, depth), None)),
        out_specs=P((*row, *col, depth), None),
        check_vma=False,
    )
```

```python
import functools

import jax
import jax.numpy as jnp
from jax import lax
from jax.experimental import pallas as pl
from jax.experimental.pallas import tpu as pltpu
from jax.sharding import Mesh, PartitionSpec as P

X = 4
Y = 8
CORES = 2
Z = 12
ZH = 2
ROWS = 64
SRC = 256
CLS = 256
HELD = CLS // (Y * CORES)
TGT = Z * ROWS
SEG = TGT // ZH
TILE = 128
STEP = 8.0
TOP = 32000.0
MIB = 1 << 20


def mask_kernel(steps, mask_hbm, a_hbm, *refs):
    n = len(steps)
    o_refs, (mask_ref, a_ref, sems) = refs[:n], refs[-3:]
    me = lax.axis_index("x")
    mask_copy = pltpu.make_async_copy(mask_hbm, mask_ref, sems.at[0])
    mask_copy.start()
    copies = []
    for b, (k, zh) in enumerate((k, zh) for k in steps for zh in range(ZH)):
        first = (zh * X + lax.rem(me + k, X)) * (SEG // TILE)
        columns = pl.ds(pl.multiple_of(first * TILE, TILE), SEG)
        copy = pltpu.make_async_copy(a_hbm.at[:, columns], a_ref.at[b], sems.at[1 + b])
        copy.start()
        copies.append((b, zh, first, copy))
    mask_copy.wait()
    for b, zh, first, copy in copies:
        copy.wait()
        for i in range(SRC // TILE):
            rows = slice(i * TILE, (i + 1) * TILE)
            for p in range(SEG // TILE):
                tile = a_ref[b, rows, p * TILE : (p + 1) * TILE]
                to = zh * SEG + p * TILE
                o_refs[b // ZH][rows, to : to + TILE] = jnp.where(mask_ref[i, first + p] != 0, tile, 0)


def spread_kernel(steps, mask_hbm, a_hbm, f_ref, *refs):
    n = len(steps)
    refs[n][...] = jnp.broadcast_to(f_ref[...][None], refs[n].shape)
    mask_kernel(steps, mask_hbm, a_hbm, *refs[:n], *refs[n + 1 :])


def mask_blocks(steps, mask, a, feats=None, limit=60):
    n = len(steps)
    whole = pl.BlockSpec(memory_space=pltpu.VMEM)
    more = [] if feats is None else [feats]
    return pl.pallas_call(
        functools.partial(spread_kernel if more else mask_kernel, steps),
        in_specs=[pl.BlockSpec(memory_space=pl.ANY)] * 2 + [whole] * len(more),
        out_specs=[whole] * (n + len(more)),
        out_shape=[jax.ShapeDtypeStruct((SRC, TGT), jnp.bfloat16)] * n
        + [jax.ShapeDtypeStruct((X * Y, HELD, SRC), jnp.bfloat16)] * len(more),
        scratch_shapes=[
            pltpu.SMEM(mask.shape, jnp.int32),
            pltpu.VMEM((n * ZH, SRC, SEG), jnp.bfloat16),
            pltpu.SemaphoreType.DMA((1 + n * ZH,)),
        ],
        compiler_params=pltpu.CompilerParams(vmem_limit_bytes=limit * MIB),
        name="mask_blocks",
    )(mask, a, *more)


def product_kernel(me_ref, f_ref, own_ref, far_ref, up_ref, down_ref, o_ref, near_ref, sems):
    wide = 2 * TILE
    copies = []
    for i in range(TGT // wide):
        columns = pl.ds(i * wide, wide)
        for n, ref in enumerate((up_ref, down_ref)):
            copy = pltpu.make_async_copy(ref.at[:, columns], near_ref.at[n, :, columns], sems.at[i, n])
            copy.start()
            copies.append(copy)
    feats = []
    for k in (0, 2, 1, 3):
        x = lax.rem(me_ref[0] + X - k, X)
        feats.append(jnp.concatenate([f_ref[c, x, y] for y in range(Y) for c in range(CORES)], axis=0))
    lane = lax.broadcasted_iota(jnp.int32, (16, TILE), 1)
    for i in range(TGT // wide):
        columns = slice(i * wide, (i + 1) * wide)
        total = jnp.dot(feats[0], own_ref[:, columns], preferred_element_type=jnp.float32)
        total += jnp.dot(feats[1], far_ref[:, columns], preferred_element_type=jnp.float32)
        for n in range(2):
            copies[2 * i + n].wait()
            total += jnp.dot(feats[2 + n], near_ref[n, :, columns], preferred_element_type=jnp.float32)
        total = total.T
        top = jnp.max(jnp.abs(total), axis=1, keepdims=True)
        power = jnp.ceil(jnp.log2(jnp.maximum(top, 1e-30)) * STEP)
        coded = jnp.round(total * (TOP * jnp.exp2(power * (-1.0 / STEP)))).astype(jnp.int32)
        power = power.astype(jnp.int32)
        for b in range(wide // ROWS):
            z = i * (wide // ROWS) + b
            rows = slice(b * ROWS, (b + 1) * ROWS)
            o_ref[z, 0:ROWS, :] = coded[rows, 0:TILE].astype(jnp.int16)
            o_ref[z, ROWS : 2 * ROWS, :] = coded[rows, TILE : 2 * TILE].astype(jnp.int16)
            scales = jnp.zeros((16, TILE), jnp.int32)
            for k in range(4):
                at = b * ROWS + 16 * k
                scales = jnp.where(lane // 32 == k, power[at : at + 16, :], scales)
            o_ref[z, 2 * ROWS : 2 * ROWS + 16, :] = scales.astype(jnp.int16)


def product(me, feats, own, far, up, down):
    whole, anywhere = pl.BlockSpec(memory_space=pltpu.VMEM), pl.BlockSpec(memory_space=pl.ANY)
    return pl.pallas_call(
        product_kernel,
        in_specs=[pl.BlockSpec(memory_space=pltpu.SMEM)] + [whole] * 3 + [anywhere] * 2,
        out_specs=whole,
        out_shape=jax.ShapeDtypeStruct((Z, 2 * ROWS + 16, TILE), jnp.int16),
        scratch_shapes=[
            pltpu.VMEM((2, SRC, TGT), jnp.bfloat16),
            pltpu.SemaphoreType.DMA((TGT // (2 * TILE), 2)),
        ],
        compiler_params=pltpu.CompilerParams(vmem_limit_bytes=16 * MIB),
        name="product",
    )(me, feats, own, far, up, down)


def finish_kernel(q_ref, t_ref, o_ref):
    left = jnp.zeros((ROWS, TILE), jnp.float32)
    right = jnp.zeros((ROWS, TILE), jnp.float32)
    for z in range(Z):
        power = q_ref[z, 2 * ROWS : 2 * ROWS + 16, :].astype(jnp.float32)
        scale = jnp.exp2(power * (1.0 / STEP)) * (1.0 / TOP)
        scale = jnp.concatenate([scale[:, 32 * k : 32 * k + 1] for k in range(4)], axis=0)
        left += q_ref[z, 0:ROWS, :].astype(jnp.float32) * scale
        right += q_ref[z, ROWS : 2 * ROWS, :].astype(jnp.float32) * scale
    o_ref[:, 0:TILE] = 0.9 * left + 0.1 * t_ref[:, 0:TILE].astype(jnp.float32)
    o_ref[:, TILE : 2 * TILE] = 0.9 * right + 0.1 * t_ref[:, TILE : 2 * TILE].astype(jnp.float32)


def finish(coded, teleport):
    return pl.pallas_call(
        finish_kernel,
        out_shape=jax.ShapeDtypeStruct((ROWS, CLS), jnp.float32),
        compiler_params=pltpu.CompilerParams(vmem_limit_bytes=16 * MIB),
        name="finish",
    )(coded, teleport)


def shift(block, k):
    return lax.ppermute(block, "x", [(i, (i + k) % X) for i in range(X)])


def others(operands):
    mask, a, feats = operands
    copies = jnp.broadcast_to(feats[None], (X * Y, HELD, SRC))
    feats = lax.all_to_all(copies, ("x", "y"), 0, 0, tiled=True)
    feats = lax.all_gather(feats, "c", axis=0)
    up, down = mask_blocks((1, 3), mask, a, limit=16)
    own_a, _ = lax.optimization_barrier((a, up))
    (own,) = mask_blocks((0,), mask, own_a, limit=16)
    return feats, own, shift(up, 1), shift(down, 3)


def nothing(operands):
    block = jnp.zeros((SRC, TGT), jnp.bfloat16)
    return jnp.zeros((CORES, X * Y, HELD, SRC), jnp.bfloat16), block, block, block


def local(propagation, tile_mask, features, teleport):
    mask, a = tile_mask[0], propagation[0]
    (far,) = mask_blocks((2,), mask, a, limit=40)
    me = lax.axis_index("x").astype(jnp.int32)
    a, _ = lax.optimization_barrier((a, far))
    feats, own, up, down = lax.cond(me < X, others, nothing, (mask, a, features[0].T))
    feats = feats.reshape(CORES, X, Y, HELD, SRC)
    coded = product(me[None], feats, own, shift(far, 2), up, down)
    coded = lax.all_to_all(coded, ("zh", "zl"), 0, 0, tiled=True)
    return finish(coded, teleport)


def solution(mesh):
    devices = mesh.devices.reshape(Y, CORES, ZH, X, Z // ZH)
    fine = Mesh(devices, ("y", "c", "zh", "x", "zl"))
    row, col, depth = ("y", "c"), ("zh", "x"), "zl"
    spec = P(depth, col, row)
    return jax.shard_map(
        local,
        mesh=fine,
        in_specs=(spec, spec, spec, P((*row, *col, depth), None)),
        out_specs=P((*row, *col, depth), None),
        check_vma=False,
    )
```

```python
import functools

import jax
import jax.numpy as jnp
from jax import lax
from jax.experimental import pallas as pl
from jax.experimental.pallas import tpu as pltpu
from jax.sharding import Mesh, PartitionSpec as P

X = 4
Y = 8
CORES = 2
Z = 12
ZH = 2
ROWS = 64
SRC = 256
CLS = 256
HELD = CLS // (Y * CORES)
TGT = Z * ROWS
SEG = TGT // ZH
TILE = 128
STEP = 8.0
TOP = 32000.0
MIB = 1 << 20


def mask_kernel(steps, mask_hbm, a_hbm, *refs):
    n = len(steps)
    o_refs, (mask_ref, a_ref, sems) = refs[:n], refs[-3:]
    me = lax.axis_index("x")
    mask_copy = pltpu.make_async_copy(mask_hbm, mask_ref, sems.at[0])
    mask_copy.start()
    copies = []
    for b, (k, zh) in enumerate((k, zh) for k in steps for zh in range(ZH)):
        first = (zh * X + lax.rem(me + k, X)) * (SEG // TILE)
        columns = pl.ds(pl.multiple_of(first * TILE, TILE), SEG)
        copy = pltpu.make_async_copy(a_hbm.at[:, columns], a_ref.at[b], sems.at[1 + b])
        copy.start()
        copies.append((b, zh, first, copy))
    mask_copy.wait()
    for b, zh, first, copy in copies:
        copy.wait()
        for i in range(SRC // TILE):
            rows = slice(i * TILE, (i + 1) * TILE)
            for p in range(SEG // TILE):
                tile = a_ref[b, rows, p * TILE : (p + 1) * TILE]
                to = zh * SEG + p * TILE
                o_refs[b // ZH][rows, to : to + TILE] = jnp.where(mask_ref[i, first + p] != 0, tile, 0)


def spread_kernel(steps, mask_hbm, a_hbm, f_ref, *refs):
    n = len(steps)
    refs[n][...] = jnp.broadcast_to(f_ref[...][None], refs[n].shape)
    mask_kernel(steps, mask_hbm, a_hbm, *refs[:n], *refs[n + 1 :])


def mask_blocks(steps, mask, a, feats=None, limit=60):
    n = len(steps)
    whole = pl.BlockSpec(memory_space=pltpu.VMEM)
    more = [] if feats is None else [feats]
    return pl.pallas_call(
        functools.partial(spread_kernel if more else mask_kernel, steps),
        in_specs=[pl.BlockSpec(memory_space=pl.ANY)] * 2 + [whole] * len(more),
        out_specs=[whole] * (n + len(more)),
        out_shape=[jax.ShapeDtypeStruct((SRC, TGT), jnp.bfloat16)] * n
        + [jax.ShapeDtypeStruct((X * Y, HELD, SRC), jnp.bfloat16)] * len(more),
        scratch_shapes=[
            pltpu.SMEM(mask.shape, jnp.int32),
            pltpu.VMEM((n * ZH, SRC, SEG), jnp.bfloat16),
            pltpu.SemaphoreType.DMA((1 + n * ZH,)),
        ],
        compiler_params=pltpu.CompilerParams(vmem_limit_bytes=limit * MIB),
        name="mask_blocks",
    )(mask, a, *more)


def product_kernel(me_ref, f_ref, *refs):
    o_ref = refs[X]
    feats = []
    for k in range(X):
        x = lax.rem(me_ref[0] + X - k, X)
        feats.append(jnp.concatenate([f_ref[c, x, y] for y in range(Y) for c in range(CORES)], axis=0))
    lane = lax.broadcasted_iota(jnp.int32, (16, TILE), 1)
    wide = 2 * TILE
    for i in range(TGT // wide):
        total = jnp.zeros((CLS, wide), jnp.float32)
        for k in range(X):
            total += jnp.dot(
                feats[k], refs[k][:, i * wide : (i + 1) * wide], preferred_element_type=jnp.float32
            )
        total = total.T
        top = jnp.max(jnp.abs(total), axis=1, keepdims=True)
        power = jnp.ceil(jnp.log2(jnp.maximum(top, 1e-30)) * STEP)
        coded = jnp.round(total * (TOP * jnp.exp2(power * (-1.0 / STEP)))).astype(jnp.int32)
        power = power.astype(jnp.int32)
        for b in range(wide // ROWS):
            z = i * (wide // ROWS) + b
            rows = slice(b * ROWS, (b + 1) * ROWS)
            o_ref[z, 0:ROWS, :] = coded[rows, 0:TILE].astype(jnp.int16)
            o_ref[z, ROWS : 2 * ROWS, :] = coded[rows, TILE : 2 * TILE].astype(jnp.int16)
            scales = jnp.zeros((16, TILE), jnp.int32)
            for k in range(4):
                at = b * ROWS + 16 * k
                scales = jnp.where(lane // 32 == k, power[at : at + 16, :], scales)
            o_ref[z, 2 * ROWS : 2 * ROWS + 16, :] = scales.astype(jnp.int16)


def product(me, feats, blocks):
    whole = pl.BlockSpec(memory_space=pltpu.VMEM)
    return pl.pallas_call(
        product_kernel,
        in_specs=[pl.BlockSpec(memory_space=pltpu.SMEM)] + [whole] * (1 + X),
        out_specs=whole,
        out_shape=jax.ShapeDtypeStruct((Z, 2 * ROWS + 16, TILE), jnp.int16),
        compiler_params=pltpu.CompilerParams(vmem_limit_bytes=8 * MIB),
        name="product",
    )(me, feats, *blocks)


def finish_kernel(q_ref, t_ref, o_ref):
    left = jnp.zeros((ROWS, TILE), jnp.float32)
    right = jnp.zeros((ROWS, TILE), jnp.float32)
    for z in range(Z):
        power = q_ref[z, 2 * ROWS : 2 * ROWS + 16, :].astype(jnp.float32)
        scale = jnp.exp2(power * (1.0 / STEP)) * (1.0 / TOP)
        scale = jnp.concatenate([scale[:, 32 * k : 32 * k + 1] for k in range(4)], axis=0)
        left += q_ref[z, 0:ROWS, :].astype(jnp.float32) * scale
        right += q_ref[z, ROWS : 2 * ROWS, :].astype(jnp.float32) * scale
    o_ref[:, 0:TILE] = 0.9 * left + 0.1 * t_ref[:, 0:TILE].astype(jnp.float32)
    o_ref[:, TILE : 2 * TILE] = 0.9 * right + 0.1 * t_ref[:, TILE : 2 * TILE].astype(jnp.float32)


def finish(coded, teleport):
    return pl.pallas_call(
        finish_kernel,
        out_shape=jax.ShapeDtypeStruct((ROWS, CLS), jnp.float32),
        compiler_params=pltpu.CompilerParams(vmem_limit_bytes=16 * MIB),
        name="finish",
    )(coded, teleport)


def shift(block, k):
    return lax.ppermute(block, "x", [(i, (i + k) % X) for i in range(X)])


def others(operands):
    mask, a, feats = operands
    copies = jnp.broadcast_to(feats[None], (X * Y, HELD, SRC))
    feats = lax.all_to_all(copies, ("x", "y"), 0, 0, tiled=True)
    feats = lax.all_gather(feats, "c", axis=0)
    up, down = mask_blocks((1, 3), mask, a, limit=16)
    own_a, _ = lax.optimization_barrier((a, up))
    (own,) = mask_blocks((0,), mask, own_a, limit=16)
    return feats, own, shift(up, 1), shift(down, 3)


def nothing(operands):
    block = jnp.zeros((SRC, TGT), jnp.bfloat16)
    return jnp.zeros((CORES, X * Y, HELD, SRC), jnp.bfloat16), block, block, block


def local(propagation, tile_mask, features, teleport):
    mask, a = tile_mask[0], propagation[0]
    (far,) = mask_blocks((2,), mask, a, limit=40)
    me = lax.axis_index("x").astype(jnp.int32)
    a, _ = lax.optimization_barrier((a, far))
    feats, own, up, down = lax.cond(me < X, others, nothing, (mask, a, features[0].T))
    feats = feats.reshape(CORES, X, Y, HELD, SRC)
    coded = product(me[None], feats, [own, up, shift(far, 2), down])
    coded = lax.all_to_all(coded, ("zh", "zl"), 0, 0, tiled=True)
    return finish(coded, teleport)


def solution(mesh):
    devices = mesh.devices.reshape(Y, CORES, ZH, X, Z // ZH)
    fine = Mesh(devices, ("y", "c", "zh", "x", "zl"))
    row, col, depth = ("y", "c"), ("zh", "x"), "zl"
    spec = P(depth, col, row)
    return jax.shard_map(
        local,
        mesh=fine,
        in_specs=(spec, spec, spec, P((*row, *col, depth), None)),
        out_specs=P((*row, *col, depth), None),
        check_vma=False,
    )
```

```python
import functools

import jax
import jax.numpy as jnp
from jax import lax
from jax.experimental import pallas as pl
from jax.experimental.pallas import tpu as pltpu
from jax.sharding import Mesh, PartitionSpec as P

X = 4
Y = 8
CORES = 2
Z = 12
ZH = 2
ROWS = 64
SRC = 256
CLS = 256
HELD = CLS // (Y * CORES)
TGT = Z * ROWS
SEG = TGT // ZH
TILE = 128
STEP = 8.0
TOP = 32000.0
MIB = 1 << 20


def mask_kernel(steps, mask_hbm, a_hbm, *refs):
    n = len(steps)
    o_refs, (mask_ref, a_ref, sems) = refs[:n], refs[-3:]
    me = lax.axis_index("x")
    mask_copy = pltpu.make_async_copy(mask_hbm, mask_ref, sems.at[0])
    mask_copy.start()
    copies = []
    for b, (k, zh) in enumerate((k, zh) for k in steps for zh in range(ZH)):
        first = (zh * X + lax.rem(me + k, X)) * (SEG // TILE)
        columns = pl.ds(pl.multiple_of(first * TILE, TILE), SEG)
        copy = pltpu.make_async_copy(a_hbm.at[:, columns], a_ref.at[b], sems.at[1 + b])
        copy.start()
        copies.append((b, zh, first, copy))
    mask_copy.wait()
    for b, zh, first, copy in copies:
        copy.wait()
        for i in range(SRC // TILE):
            rows = slice(i * TILE, (i + 1) * TILE)
            for p in range(SEG // TILE):
                tile = a_ref[b, rows, p * TILE : (p + 1) * TILE]
                to = zh * SEG + p * TILE
                o_refs[b // ZH][rows, to : to + TILE] = jnp.where(mask_ref[i, first + p] != 0, tile, 0)


def spread_kernel(steps, mask_hbm, a_hbm, f_ref, *refs):
    n = len(steps)
    refs[n][...] = jnp.broadcast_to(f_ref[...][None], refs[n].shape)
    mask_kernel(steps, mask_hbm, a_hbm, *refs[:n], *refs[n + 1 :])


def mask_blocks(steps, mask, a, feats=None, limit=60):
    n = len(steps)
    whole = pl.BlockSpec(memory_space=pltpu.VMEM)
    more = [] if feats is None else [feats]
    return pl.pallas_call(
        functools.partial(spread_kernel if more else mask_kernel, steps),
        in_specs=[pl.BlockSpec(memory_space=pl.ANY)] * 2 + [whole] * len(more),
        out_specs=[whole] * (n + len(more)),
        out_shape=[jax.ShapeDtypeStruct((SRC, TGT), jnp.bfloat16)] * n
        + [jax.ShapeDtypeStruct((X * Y, HELD, SRC), jnp.bfloat16)] * len(more),
        scratch_shapes=[
            pltpu.SMEM(mask.shape, jnp.int32),
            pltpu.VMEM((n * ZH, SRC, SEG), jnp.bfloat16),
            pltpu.SemaphoreType.DMA((1 + n * ZH,)),
        ],
        compiler_params=pltpu.CompilerParams(vmem_limit_bytes=limit * MIB),
        name="mask_blocks",
    )(mask, a, *more)


def product_kernel(me_ref, f_ref, *refs):
    o_ref = refs[X]
    feats = []
    for k in range(X):
        x = lax.rem(me_ref[0] + X - k, X)
        feats.append(jnp.concatenate([f_ref[c, x, y] for y in range(Y) for c in range(CORES)], axis=0))
    lane = lax.broadcasted_iota(jnp.int32, (16, TILE), 1)
    wide = 2 * TILE
    for i in range(TGT // wide):
        total = jnp.zeros((CLS, wide), jnp.float32)
        for k in range(X):
            total += jnp.dot(
                feats[k], refs[k][:, i * wide : (i + 1) * wide], preferred_element_type=jnp.float32
            )
        total = total.T
        top = jnp.max(jnp.abs(total), axis=1, keepdims=True)
        power = jnp.ceil(jnp.log2(jnp.maximum(top, 1e-30)) * STEP)
        coded = jnp.round(total * (TOP * jnp.exp2(power * (-1.0 / STEP)))).astype(jnp.int32)
        power = power.astype(jnp.int32)
        for b in range(wide // ROWS):
            z = i * (wide // ROWS) + b
            rows = slice(b * ROWS, (b + 1) * ROWS)
            o_ref[z, 0:ROWS, :] = coded[rows, 0:TILE].astype(jnp.int16)
            o_ref[z, ROWS : 2 * ROWS, :] = coded[rows, TILE : 2 * TILE].astype(jnp.int16)
            scales = jnp.zeros((16, TILE), jnp.int32)
            for k in range(4):
                at = b * ROWS + 16 * k
                scales = jnp.where(lane // 32 == k, power[at : at + 16, :], scales)
            o_ref[z, 2 * ROWS : 2 * ROWS + 16, :] = scales.astype(jnp.int16)


def product(me, feats, blocks):
    whole = pl.BlockSpec(memory_space=pltpu.VMEM)
    return pl.pallas_call(
        product_kernel,
        in_specs=[pl.BlockSpec(memory_space=pltpu.SMEM)] + [whole] * (1 + X),
        out_specs=whole,
        out_shape=jax.ShapeDtypeStruct((Z, 2 * ROWS + 16, TILE), jnp.int16),
        compiler_params=pltpu.CompilerParams(vmem_limit_bytes=8 * MIB),
        name="product",
    )(me, feats, *blocks)


def finish_kernel(q_ref, t_ref, o_ref):
    left = jnp.zeros((ROWS, TILE), jnp.float32)
    right = jnp.zeros((ROWS, TILE), jnp.float32)
    for z in range(Z):
        power = q_ref[z, 2 * ROWS : 2 * ROWS + 16, :].astype(jnp.float32)
        scale = jnp.exp2(power * (1.0 / STEP)) * (1.0 / TOP)
        scale = jnp.concatenate([scale[:, 32 * k : 32 * k + 1] for k in range(4)], axis=0)
        left += q_ref[z, 0:ROWS, :].astype(jnp.float32) * scale
        right += q_ref[z, ROWS : 2 * ROWS, :].astype(jnp.float32) * scale
    o_ref[:, 0:TILE] = 0.9 * left + 0.1 * t_ref[:, 0:TILE].astype(jnp.float32)
    o_ref[:, TILE : 2 * TILE] = 0.9 * right + 0.1 * t_ref[:, TILE : 2 * TILE].astype(jnp.float32)


def finish(coded, teleport):
    return pl.pallas_call(
        finish_kernel,
        out_shape=jax.ShapeDtypeStruct((ROWS, CLS), jnp.float32),
        compiler_params=pltpu.CompilerParams(vmem_limit_bytes=16 * MIB),
        name="finish",
    )(coded, teleport)


def shift(block, k):
    return lax.ppermute(block, "x", [(i, (i + k) % X) for i in range(X)])


def others(operands):
    mask, a, feats = operands
    copies = jnp.broadcast_to(feats[None], (X * Y, HELD, SRC))
    feats = lax.all_to_all(copies, ("x", "y"), 0, 0, tiled=True)
    feats = lax.all_gather(feats, "c", axis=0)
    (down,) = mask_blocks((3,), mask, a, limit=16)
    own_a, _ = lax.optimization_barrier((a, down))
    (own,) = mask_blocks((0,), mask, own_a, limit=16)
    return feats, own, shift(down, 3)


def nothing(operands):
    block = jnp.zeros((SRC, TGT), jnp.bfloat16)
    return jnp.zeros((CORES, X * Y, HELD, SRC), jnp.bfloat16), block, block


def local(propagation, tile_mask, features, teleport):
    mask, a = tile_mask[0], propagation[0]
    far, up = mask_blocks((2, 1), mask, a, limit=40)
    me = lax.axis_index("x").astype(jnp.int32)
    a, _ = lax.optimization_barrier((a, far))
    feats, own, down = lax.cond(me < X, others, nothing, (mask, a, features[0].T))
    feats = feats.reshape(CORES, X, Y, HELD, SRC)
    coded = product(me[None], feats, [own, shift(up, 1), shift(far, 2), down])
    coded = lax.all_to_all(coded, ("zh", "zl"), 0, 0, tiled=True)
    return finish(coded, teleport)


def solution(mesh):
    devices = mesh.devices.reshape(Y, CORES, ZH, X, Z // ZH)
    fine = Mesh(devices, ("y", "c", "zh", "x", "zl"))
    row, col, depth = ("y", "c"), ("zh", "x"), "zl"
    spec = P(depth, col, row)
    return jax.shard_map(
        local,
        mesh=fine,
        in_specs=(spec, spec, spec, P((*row, *col, depth), None)),
        out_specs=P((*row, *col, depth), None),
        check_vma=False,
    )
```

```python
import functools

import jax
import jax.numpy as jnp
from jax import lax
from jax.experimental import pallas as pl
from jax.experimental.pallas import tpu as pltpu
from jax.sharding import Mesh, PartitionSpec as P

X = 4
Y = 8
CORES = 2
Z = 12
ZH = 2
ROWS = 64
SRC = 256
CLS = 256
HELD = CLS // (Y * CORES)
TGT = Z * ROWS
SEG = TGT // ZH
TILE = 128
SUB = 8
STEP = 8.0
TOP = 32000.0
MIB = 1 << 20


def mask_kernel(steps, mask_hbm, a_hbm, *refs):
    n = len(steps)
    o_refs, (mask_ref, a_ref, sems) = refs[:n], refs[-3:]
    me = lax.axis_index("x")
    mask_copy = pltpu.make_async_copy(mask_hbm, mask_ref, sems.at[0])
    mask_copy.start()
    copies = []
    for b, (k, zh) in enumerate((k, zh) for k in steps for zh in range(ZH)):
        first = (zh * X + lax.rem(me + k, X)) * (SEG // TILE)
        columns = pl.ds(pl.multiple_of(first * TILE, TILE), SEG)
        copy = pltpu.make_async_copy(a_hbm.at[:, columns], a_ref.at[b], sems.at[1 + b])
        copy.start()
        copies.append((b, zh, first, copy))
    mask_copy.wait()
    for b, zh, first, copy in copies:
        copy.wait()
        for i in range(SRC // TILE):
            rows = slice(i * TILE, (i + 1) * TILE)
            for p in range(SEG // TILE):
                tile = a_ref[b, rows, p * TILE : (p + 1) * TILE]
                to = zh * SEG + p * TILE
                o_refs[b // ZH][rows, to : to + TILE] = jnp.where(mask_ref[i, first + p] != 0, tile, 0)


def spread_kernel(steps, mask_hbm, a_hbm, f_ref, *refs):
    n = len(steps)
    refs[n][...] = jnp.broadcast_to(f_ref[...][None], refs[n].shape)
    mask_kernel(steps, mask_hbm, a_hbm, *refs[:n], *refs[n + 1 :])


def mask_blocks(steps, mask, a, feats=None, limit=60):
    n = len(steps)
    whole = pl.BlockSpec(memory_space=pltpu.VMEM)
    more = [] if feats is None else [feats]
    return pl.pallas_call(
        functools.partial(spread_kernel if more else mask_kernel, steps),
        in_specs=[pl.BlockSpec(memory_space=pl.ANY)] * 2 + [whole] * len(more),
        out_specs=[whole] * (n + len(more)),
        out_shape=[jax.ShapeDtypeStruct((SRC, TGT), jnp.bfloat16)] * n
        + [jax.ShapeDtypeStruct((X * Y, HELD, SRC), jnp.bfloat16)] * len(more),
        scratch_shapes=[
            pltpu.SMEM(mask.shape, jnp.int32),
            pltpu.VMEM((n * ZH, SRC, SEG), jnp.bfloat16),
            pltpu.SemaphoreType.DMA((1 + n * ZH,)),
        ],
        compiler_params=pltpu.CompilerParams(vmem_limit_bytes=limit * MIB),
        name="mask_blocks",
    )(mask, a, *more)


def product_kernel(me_ref, f_ref, *refs):
    o_ref = refs[X]
    feats = []
    for k in range(X):
        x = lax.rem(me_ref[0] + X - k, X)
        feats.append(jnp.concatenate([f_ref[c, x, y] for y in range(Y) for c in range(CORES)], axis=0))
    lane = lax.broadcasted_iota(jnp.int32, (SUB, TILE), 1)
    wide = 2 * TILE
    for i in range(TGT // wide):
        total = jnp.zeros((CLS, wide), jnp.float32)
        for k in range(X):
            total += jnp.dot(
                feats[k], refs[k][:, i * wide : (i + 1) * wide], preferred_element_type=jnp.float32
            )
        total = total.T
        top = jnp.max(jnp.abs(total), axis=1, keepdims=True)
        power = jnp.ceil(jnp.log2(jnp.maximum(top, 1e-30)) * STEP)
        coded = jnp.round(total * (TOP * jnp.exp2(power * (-1.0 / STEP)))).astype(jnp.int32)
        power = power.astype(jnp.int32)
        for b in range(wide // ROWS):
            z = i * (wide // ROWS) + b
            rows = slice(b * ROWS, (b + 1) * ROWS)
            o_ref[z, 0:ROWS, :] = coded[rows, 0:TILE].astype(jnp.int16)
            o_ref[z, ROWS : 2 * ROWS, :] = coded[rows, TILE : 2 * TILE].astype(jnp.int16)
            scales = jnp.zeros((SUB, TILE), jnp.int32)
            for k in range(ROWS // SUB):
                at = b * ROWS + SUB * k
                scales = jnp.where(lane // (TILE * SUB // ROWS) == k, power[at : at + SUB, :], scales)
            o_ref[z, 2 * ROWS : 2 * ROWS + SUB, :] = scales.astype(jnp.int16)


def product(me, feats, blocks):
    whole = pl.BlockSpec(memory_space=pltpu.VMEM)
    return pl.pallas_call(
        product_kernel,
        in_specs=[pl.BlockSpec(memory_space=pltpu.SMEM)] + [whole] * (1 + X),
        out_specs=whole,
        out_shape=jax.ShapeDtypeStruct((Z, 2 * ROWS + SUB, TILE), jnp.int16),
        compiler_params=pltpu.CompilerParams(vmem_limit_bytes=8 * MIB),
        name="product",
    )(me, feats, *blocks)


def finish_kernel(q_ref, t_ref, o_ref):
    left = jnp.zeros((ROWS, TILE), jnp.float32)
    right = jnp.zeros((ROWS, TILE), jnp.float32)
    for z in range(Z):
        power = q_ref[z, 2 * ROWS : 2 * ROWS + SUB, :].astype(jnp.float32)
        scale = jnp.exp2(power * (1.0 / STEP)) * (1.0 / TOP)
        step = TILE * SUB // ROWS
        scale = jnp.concatenate([scale[:, k : k + 1] for k in range(0, TILE, step)], axis=0)
        left += q_ref[z, 0:ROWS, :].astype(jnp.float32) * scale
        right += q_ref[z, ROWS : 2 * ROWS, :].astype(jnp.float32) * scale
    o_ref[:, 0:TILE] = 0.9 * left + 0.1 * t_ref[:, 0:TILE].astype(jnp.float32)
    o_ref[:, TILE : 2 * TILE] = 0.9 * right + 0.1 * t_ref[:, TILE : 2 * TILE].astype(jnp.float32)


def finish(coded, teleport):
    return pl.pallas_call(
        finish_kernel,
        out_shape=jax.ShapeDtypeStruct((ROWS, CLS), jnp.float32),
        compiler_params=pltpu.CompilerParams(vmem_limit_bytes=16 * MIB),
        name="finish",
    )(coded, teleport)


def shift(block, k):
    return lax.ppermute(block, "x", [(i, (i + k) % X) for i in range(X)])


def others(operands):
    mask, a, feats = operands
    copies = jnp.broadcast_to(feats[None], (X * Y, HELD, SRC))
    feats = lax.all_to_all(copies, ("x", "y"), 0, 0, tiled=True)
    feats = lax.all_gather(feats, "c", axis=0)
    up, down = mask_blocks((1, 3), mask, a, limit=16)
    own_a, _ = lax.optimization_barrier((a, up))
    (own,) = mask_blocks((0,), mask, own_a, limit=16)
    return feats, own, shift(up, 1), shift(down, 3)


def nothing(operands):
    block = jnp.zeros((SRC, TGT), jnp.bfloat16)
    return jnp.zeros((CORES, X * Y, HELD, SRC), jnp.bfloat16), block, block, block


def local(propagation, tile_mask, features, teleport):
    mask, a = tile_mask[0], propagation[0]
    (far,) = mask_blocks((2,), mask, a, limit=40)
    me = lax.axis_index("x").astype(jnp.int32)
    a, _ = lax.optimization_barrier((a, far))
    feats, own, up, down = lax.cond(me < X, others, nothing, (mask, a, features[0].T))
    feats = feats.reshape(CORES, X, Y, HELD, SRC)
    coded = product(me[None], feats, [own, up, shift(far, 2), down])
    coded = lax.all_to_all(coded, ("zh", "zl"), 0, 0, tiled=True)
    return finish(coded, teleport)


def solution(mesh):
    devices = mesh.devices.reshape(Y, CORES, ZH, X, Z // ZH)
    fine = Mesh(devices, ("y", "c", "zh", "x", "zl"))
    row, col, depth = ("y", "c"), ("zh", "x"), "zl"
    spec = P(depth, col, row)
    return jax.shard_map(
        local,
        mesh=fine,
        in_specs=(spec, spec, spec, P((*row, *col, depth), None)),
        out_specs=P((*row, *col, depth), None),
        check_vma=False,
    )
```

```python
import functools

import jax
import jax.numpy as jnp
from jax import lax
from jax.experimental import pallas as pl
from jax.experimental.pallas import tpu as pltpu
from jax.sharding import Mesh, PartitionSpec as P

X = 4
Y = 8
CORES = 2
Z = 12
ZH = 2
ROWS = 64
SRC = 256
CLS = 256
HELD = CLS // (Y * CORES)
TGT = Z * ROWS
SEG = TGT // ZH
TILE = 128
SUB = 8
STEP = 8.0
TOP = 32000.0
MIB = 1 << 20


def mask_kernel(steps, mask_hbm, a_hbm, *refs):
    n = len(steps)
    o_refs, (mask_ref, a_ref, sems) = refs[:n], refs[-3:]
    me = lax.axis_index("x")
    mask_copy = pltpu.make_async_copy(mask_hbm, mask_ref, sems.at[0])
    mask_copy.start()
    copies = []
    for b, (k, zh) in enumerate((k, zh) for k in steps for zh in range(ZH)):
        first = (zh * X + lax.rem(me + k, X)) * (SEG // TILE)
        columns = pl.ds(pl.multiple_of(first * TILE, TILE), SEG)
        copy = pltpu.make_async_copy(a_hbm.at[:, columns], a_ref.at[b], sems.at[1 + b])
        copy.start()
        copies.append((b, zh, first, copy))
    mask_copy.wait()
    for b, zh, first, copy in copies:
        copy.wait()
        for i in range(SRC // TILE):
            rows = slice(i * TILE, (i + 1) * TILE)
            for p in range(SEG // TILE):
                tile = a_ref[b, rows, p * TILE : (p + 1) * TILE]
                to = zh * SEG + p * TILE
                o_refs[b // ZH][rows, to : to + TILE] = jnp.where(mask_ref[i, first + p] != 0, tile, 0)


def spread_kernel(steps, mask_hbm, a_hbm, f_ref, *refs):
    n = len(steps)
    refs[n][...] = jnp.broadcast_to(f_ref[...][None], refs[n].shape)
    mask_kernel(steps, mask_hbm, a_hbm, *refs[:n], *refs[n + 1 :])


def mask_blocks(steps, mask, a, feats=None, limit=60):
    n = len(steps)
    whole = pl.BlockSpec(memory_space=pltpu.VMEM)
    more = [] if feats is None else [feats]
    return pl.pallas_call(
        functools.partial(spread_kernel if more else mask_kernel, steps),
        in_specs=[pl.BlockSpec(memory_space=pl.ANY)] * 2 + [whole] * len(more),
        out_specs=[whole] * (n + len(more)),
        out_shape=[jax.ShapeDtypeStruct((SRC, TGT), jnp.bfloat16)] * n
        + [jax.ShapeDtypeStruct((X * Y, HELD, SRC), jnp.bfloat16)] * len(more),
        scratch_shapes=[
            pltpu.SMEM(mask.shape, jnp.int32),
            pltpu.VMEM((n * ZH, SRC, SEG), jnp.bfloat16),
            pltpu.SemaphoreType.DMA((1 + n * ZH,)),
        ],
        compiler_params=pltpu.CompilerParams(vmem_limit_bytes=limit * MIB),
        name="mask_blocks",
    )(mask, a, *more)


def product_kernel(me_ref, f_ref, own_ref, far_ref, up_ref, down_ref, o_ref, near_ref, total_ref, sems):
    copies = [
        pltpu.make_async_copy(ref, near_ref.at[n], sems.at[n]) for n, ref in enumerate((up_ref, down_ref))
    ]
    for copy in copies:
        copy.start()
    feats = []
    for k in (0, 2, 1, 3):
        x = lax.rem(me_ref[0] + X - k, X)
        feats.append(jnp.concatenate([f_ref[c, x, y] for y in range(Y) for c in range(CORES)], axis=0))
    lane = lax.broadcasted_iota(jnp.int32, (SUB, TILE), 1)
    wide = 2 * TILE
    for i in range(TGT // wide):
        columns = slice(i * wide, (i + 1) * wide)
        total = jnp.dot(feats[0], own_ref[:, columns], preferred_element_type=jnp.float32)
        total += jnp.dot(feats[1], far_ref[:, columns], preferred_element_type=jnp.float32)
        total_ref[i] = total
    for copy in copies:
        copy.wait()
    for i in range(TGT // wide):
        columns = slice(i * wide, (i + 1) * wide)
        total = total_ref[i]
        for n in range(2):
            total += jnp.dot(feats[2 + n], near_ref[n, :, columns], preferred_element_type=jnp.float32)
        total = total.T
        top = jnp.max(jnp.abs(total), axis=1, keepdims=True)
        power = jnp.ceil(jnp.log2(jnp.maximum(top, 1e-30)) * STEP)
        coded = jnp.round(total * (TOP * jnp.exp2(power * (-1.0 / STEP)))).astype(jnp.int32)
        power = power.astype(jnp.int32)
        for b in range(wide // ROWS):
            z = i * (wide // ROWS) + b
            rows = slice(b * ROWS, (b + 1) * ROWS)
            o_ref[z, 0:ROWS, :] = coded[rows, 0:TILE].astype(jnp.int16)
            o_ref[z, ROWS : 2 * ROWS, :] = coded[rows, TILE : 2 * TILE].astype(jnp.int16)
            scales = jnp.zeros((SUB, TILE), jnp.int32)
            for k in range(ROWS // SUB):
                at = b * ROWS + SUB * k
                scales = jnp.where(lane // (TILE * SUB // ROWS) == k, power[at : at + SUB, :], scales)
            o_ref[z, 2 * ROWS : 2 * ROWS + SUB, :] = scales.astype(jnp.int16)


def product(me, feats, own, far, up, down):
    whole, anywhere = pl.BlockSpec(memory_space=pltpu.VMEM), pl.BlockSpec(memory_space=pl.ANY)
    return pl.pallas_call(
        product_kernel,
        in_specs=[pl.BlockSpec(memory_space=pltpu.SMEM)] + [whole] * 3 + [anywhere] * 2,
        out_specs=whole,
        out_shape=jax.ShapeDtypeStruct((Z, 2 * ROWS + SUB, TILE), jnp.int16),
        scratch_shapes=[
            pltpu.VMEM((2, SRC, TGT), jnp.bfloat16),
            pltpu.VMEM((TGT // (2 * TILE), CLS, 2 * TILE), jnp.float32),
            pltpu.SemaphoreType.DMA((2,)),
        ],
        compiler_params=pltpu.CompilerParams(vmem_limit_bytes=8 * MIB),
        name="product",
    )(me, feats, own, far, up, down)


def finish_kernel(q_ref, t_ref, o_ref):
    left = jnp.zeros((ROWS, TILE), jnp.float32)
    right = jnp.zeros((ROWS, TILE), jnp.float32)
    for z in range(Z):
        power = q_ref[z, 2 * ROWS : 2 * ROWS + SUB, :].astype(jnp.float32)
        scale = jnp.exp2(power * (1.0 / STEP)) * (1.0 / TOP)
        step = TILE * SUB // ROWS
        scale = jnp.concatenate([scale[:, k : k + 1] for k in range(0, TILE, step)], axis=0)
        left += q_ref[z, 0:ROWS, :].astype(jnp.float32) * scale
        right += q_ref[z, ROWS : 2 * ROWS, :].astype(jnp.float32) * scale
    o_ref[:, 0:TILE] = 0.9 * left + 0.1 * t_ref[:, 0:TILE].astype(jnp.float32)
    o_ref[:, TILE : 2 * TILE] = 0.9 * right + 0.1 * t_ref[:, TILE : 2 * TILE].astype(jnp.float32)


def finish(coded, teleport):
    return pl.pallas_call(
        finish_kernel,
        out_shape=jax.ShapeDtypeStruct((ROWS, CLS), jnp.float32),
        compiler_params=pltpu.CompilerParams(vmem_limit_bytes=16 * MIB),
        name="finish",
    )(coded, teleport)


def shift(block, k):
    return lax.ppermute(block, "x", [(i, (i + k) % X) for i in range(X)])


def others(operands):
    mask, a, feats = operands
    copies = jnp.broadcast_to(feats[None], (X * Y, HELD, SRC))
    feats = lax.all_to_all(copies, ("x", "y"), 0, 0, tiled=True)
    feats = lax.all_gather(feats, "c", axis=0)
    up, down = mask_blocks((1, 3), mask, a, limit=16)
    own_a, _ = lax.optimization_barrier((a, up))
    (own,) = mask_blocks((0,), mask, own_a, limit=16)
    return feats, own, shift(up, 1), shift(down, 3)


def nothing(operands):
    block = jnp.zeros((SRC, TGT), jnp.bfloat16)
    return jnp.zeros((CORES, X * Y, HELD, SRC), jnp.bfloat16), block, block, block


def local(propagation, tile_mask, features, teleport):
    mask, a = tile_mask[0], propagation[0]
    (far,) = mask_blocks((2,), mask, a, limit=40)
    me = lax.axis_index("x").astype(jnp.int32)
    a, _ = lax.optimization_barrier((a, far))
    feats, own, up, down = lax.cond(me < X, others, nothing, (mask, a, features[0].T))
    feats = feats.reshape(CORES, X, Y, HELD, SRC)
    coded = product(me[None], feats, own, shift(far, 2), up, down)
    coded = lax.all_to_all(coded, ("zh", "zl"), 0, 0, tiled=True)
    return finish(coded, teleport)


def solution(mesh):
    devices = mesh.devices.reshape(Y, CORES, ZH, X, Z // ZH)
    fine = Mesh(devices, ("y", "c", "zh", "x", "zl"))
    row, col, depth = ("y", "c"), ("zh", "x"), "zl"
    spec = P(depth, col, row)
    return jax.shard_map(
        local,
        mesh=fine,
        in_specs=(spec, spec, spec, P((*row, *col, depth), None)),
        out_specs=P((*row, *col, depth), None),
        check_vma=False,
    )
```

```python
import functools

import jax
import jax.numpy as jnp
from jax import lax
from jax.experimental import pallas as pl
from jax.experimental.pallas import tpu as pltpu
from jax.sharding import Mesh, PartitionSpec as P

X = 4
Y = 8
CORES = 2
Z = 12
ZH = 2
ROWS = 64
SRC = 256
CLS = 256
HELD = CLS // (Y * CORES)
TGT = Z * ROWS
SEG = TGT // ZH
TILE = 128
SUB = 8
STEP = 8.0
TOP = 32000.0
MIB = 1 << 20


def mask_kernel(steps, mask_hbm, a_hbm, *refs):
    n = len(steps)
    o_refs, (mask_ref, a_ref, sems) = refs[:n], refs[-3:]
    me = lax.axis_index("x")
    mask_copy = pltpu.make_async_copy(mask_hbm, mask_ref, sems.at[0])
    mask_copy.start()
    copies = []
    for b, (k, zh) in enumerate((k, zh) for k in steps for zh in range(ZH)):
        first = (zh * X + lax.rem(me + k, X)) * (SEG // TILE)
        columns = pl.ds(pl.multiple_of(first * TILE, TILE), SEG)
        copy = pltpu.make_async_copy(a_hbm.at[:, columns], a_ref.at[b], sems.at[1 + b])
        copy.start()
        copies.append((b, zh, first, copy))
    mask_copy.wait()
    for b, zh, first, copy in copies:
        copy.wait()
        for i in range(SRC // TILE):
            rows = slice(i * TILE, (i + 1) * TILE)
            for p in range(SEG // TILE):
                tile = a_ref[b, rows, p * TILE : (p + 1) * TILE]
                to = zh * SEG + p * TILE
                o_refs[b // ZH][rows, to : to + TILE] = jnp.where(mask_ref[i, first + p] != 0, tile, 0)


def spread_kernel(steps, mask_hbm, a_hbm, f_ref, *refs):
    n = len(steps)
    refs[n][...] = jnp.broadcast_to(f_ref[...][None], refs[n].shape)
    mask_kernel(steps, mask_hbm, a_hbm, *refs[:n], *refs[n + 1 :])


def mask_blocks(steps, mask, a, feats=None, limit=60):
    n = len(steps)
    whole = pl.BlockSpec(memory_space=pltpu.VMEM)
    more = [] if feats is None else [feats]
    return pl.pallas_call(
        functools.partial(spread_kernel if more else mask_kernel, steps),
        in_specs=[pl.BlockSpec(memory_space=pl.ANY)] * 2 + [whole] * len(more),
        out_specs=[whole] * (n + len(more)),
        out_shape=[jax.ShapeDtypeStruct((SRC, TGT), jnp.bfloat16)] * n
        + [jax.ShapeDtypeStruct((X * Y, HELD, SRC), jnp.bfloat16)] * len(more),
        scratch_shapes=[
            pltpu.SMEM(mask.shape, jnp.int32),
            pltpu.VMEM((n * ZH, SRC, SEG), jnp.bfloat16),
            pltpu.SemaphoreType.DMA((1 + n * ZH,)),
        ],
        compiler_params=pltpu.CompilerParams(vmem_limit_bytes=limit * MIB),
        name="mask_blocks",
    )(mask, a, *more)


def product_kernel(me_ref, f_ref, *refs):
    o_ref = refs[X]
    feats = []
    for k in range(X):
        x = lax.rem(me_ref[0] + X - k, X)
        feats.append(jnp.concatenate([f_ref[c, y, x] for y in range(Y) for c in range(CORES)], axis=0))
    lane = lax.broadcasted_iota(jnp.int32, (SUB, TILE), 1)
    wide = 2 * TILE
    for i in range(TGT // wide):
        total = jnp.zeros((CLS, wide), jnp.float32)
        for k in range(X):
            total += jnp.dot(
                feats[k], refs[k][:, i * wide : (i + 1) * wide], preferred_element_type=jnp.float32
            )
        total = total.T
        top = jnp.max(jnp.abs(total), axis=1, keepdims=True)
        power = jnp.ceil(jnp.log2(jnp.maximum(top, 1e-30)) * STEP)
        coded = jnp.round(total * (TOP * jnp.exp2(power * (-1.0 / STEP)))).astype(jnp.int32)
        power = power.astype(jnp.int32)
        for b in range(wide // ROWS):
            z = i * (wide // ROWS) + b
            rows = slice(b * ROWS, (b + 1) * ROWS)
            o_ref[z, 0:ROWS, :] = coded[rows, 0:TILE].astype(jnp.int16)
            o_ref[z, ROWS : 2 * ROWS, :] = coded[rows, TILE : 2 * TILE].astype(jnp.int16)
            scales = jnp.zeros((SUB, TILE), jnp.int32)
            for k in range(ROWS // SUB):
                at = b * ROWS + SUB * k
                scales = jnp.where(lane // (TILE * SUB // ROWS) == k, power[at : at + SUB, :], scales)
            o_ref[z, 2 * ROWS : 2 * ROWS + SUB, :] = scales.astype(jnp.int16)


def product(me, feats, blocks):
    whole = pl.BlockSpec(memory_space=pltpu.VMEM)
    return pl.pallas_call(
        product_kernel,
        in_specs=[pl.BlockSpec(memory_space=pltpu.SMEM)] + [whole] * (1 + X),
        out_specs=whole,
        out_shape=jax.ShapeDtypeStruct((Z, 2 * ROWS + SUB, TILE), jnp.int16),
        compiler_params=pltpu.CompilerParams(vmem_limit_bytes=8 * MIB),
        name="product",
    )(me, feats, *blocks)


def finish_kernel(q_ref, t_ref, o_ref):
    left = jnp.zeros((ROWS, TILE), jnp.float32)
    right = jnp.zeros((ROWS, TILE), jnp.float32)
    for z in range(Z):
        power = q_ref[z, 2 * ROWS : 2 * ROWS + SUB, :].astype(jnp.float32)
        scale = jnp.exp2(power * (1.0 / STEP)) * (1.0 / TOP)
        step = TILE * SUB // ROWS
        scale = jnp.concatenate([scale[:, k : k + 1] for k in range(0, TILE, step)], axis=0)
        left += q_ref[z, 0:ROWS, :].astype(jnp.float32) * scale
        right += q_ref[z, ROWS : 2 * ROWS, :].astype(jnp.float32) * scale
    o_ref[:, 0:TILE] = 0.9 * left + 0.1 * t_ref[:, 0:TILE].astype(jnp.float32)
    o_ref[:, TILE : 2 * TILE] = 0.9 * right + 0.1 * t_ref[:, TILE : 2 * TILE].astype(jnp.float32)


def finish(coded, teleport):
    return pl.pallas_call(
        finish_kernel,
        out_shape=jax.ShapeDtypeStruct((ROWS, CLS), jnp.float32),
        compiler_params=pltpu.CompilerParams(vmem_limit_bytes=16 * MIB),
        name="finish",
    )(coded, teleport)


def shift(block, k):
    return lax.ppermute(block, "x", [(i, (i + k) % X) for i in range(X)])


def others(operands):
    mask, a, feats = operands
    copies = jnp.broadcast_to(feats[None], (X * Y, HELD, SRC))
    feats = lax.all_to_all(copies, ("y", "x"), 0, 0, tiled=True)
    feats = lax.all_gather(feats, "c", axis=0)
    up, down = mask_blocks((1, 3), mask, a, limit=16)
    own_a, _ = lax.optimization_barrier((a, up))
    (own,) = mask_blocks((0,), mask, own_a, limit=16)
    return feats, own, shift(up, 1), shift(down, 3)


def nothing(operands):
    block = jnp.zeros((SRC, TGT), jnp.bfloat16)
    return jnp.zeros((CORES, X * Y, HELD, SRC), jnp.bfloat16), block, block, block


def local(propagation, tile_mask, features, teleport):
    mask, a = tile_mask[0], propagation[0]
    (far,) = mask_blocks((2,), mask, a, limit=40)
    me = lax.axis_index("x").astype(jnp.int32)
    a, _ = lax.optimization_barrier((a, far))
    feats, own, up, down = lax.cond(me < X, others, nothing, (mask, a, features[0].T))
    feats = feats.reshape(CORES, Y, X, HELD, SRC)
    coded = product(me[None], feats, [own, up, shift(far, 2), down])
    coded = lax.all_to_all(coded, ("zh", "zl"), 0, 0, tiled=True)
    return finish(coded, teleport)


def solution(mesh):
    devices = mesh.devices.reshape(Y, CORES, ZH, X, Z // ZH)
    fine = Mesh(devices, ("y", "c", "zh", "x", "zl"))
    row, col, depth = ("y", "c"), ("zh", "x"), "zl"
    spec = P(depth, col, row)
    return jax.shard_map(
        local,
        mesh=fine,
        in_specs=(spec, spec, spec, P((*row, *col, depth), None)),
        out_specs=P((*row, *col, depth), None),
        check_vma=False,
    )
```
